32 devices in a mesh: seq: 8 (over z, y), tp: 4 (over x, core).
Axes of the slice: x: 2, y: 2, z: 4, core: 2. Of those that a mesh axis runs over, the one named last changes fastest.
Arguments:
- normed: bfloat16 [4096, 2048], P('seq', 'tp'), may hold values from -24 to 24
- cluster: int32 [4096, 1], P('seq'), may hold values from 0 to 127; in each aligned block of 512 rows (0 to 511, 512 to 1023, ...) at most 8 rows name the same one
- w_query: bfloat16 [2048, 2048], P(None, 'tp'), may hold values from -1 to 1
- w_key: bfloat16 [2048, 2048], P(None, 'tp'), may hold values from -1 to 1
- w_value: bfloat16 [2048, 2048], P(None, 'tp'), may hold values from -0.125 to 0.125
- w_out: bfloat16 [2048, 2048], P('tp'), may hold values from -0.125 to 0.125
- grad_out: bfloat16 [4096, 2048], P('seq', 'tp'), may hold values from -6 to 6
Outputs:
- attended: bfloat16 [4096, 2048], P('seq', 'tp')
- grad_normed: float32 [4096, 2048], P('seq', 'tp')
The draws below stay inside these ranges and needn't reach their ends.
Inputs may be any that keep to these rules, and one draw needn't show every extreme that they name: Among the tokens of one index of seq no cluster id appears more than 8 times, and some id appears exactly 8 times; every id appears somewhere.
All inputs are finite; a program needn't handle non-finite values.
Results may differ from the reference program's by a relative error of at most 0.011.
The reference program's roundings to bfloat16 on the way count: a program that leaves them out, or rounds other values in their place, can miss the bound.
Values may be sent and summed in bfloat16 or wider, within the bound.
No kernel may reach another device: no remote copies, remote signals or barrier semaphores. Data moves between devices by JAX's collectives and lax.ppermute only.
A program may use at most 128 MiB of HBM per device.

```python
import math
import jax
import jax.numpy as jnp
import numpy as np
from jax import lax

D = 2048
HEADS = 16
HEAD_DIM = 128
CLUSTERS = 128
CAP = 256
TOK_DEV = 512
TOKENS = 4096
MOST = 8


def weight_pair(key):
    first = jax.random.normal(jax.random.fold_in(key, 11), (D, D), jnp.float32)
    second = jax.random.normal(jax.random.fold_in(key, 12), (D, D), jnp.float32)
    first = jnp.clip(first, -5.5, 5.5) / math.sqrt(D)
    second = jnp.clip(second, -5.5, 5.5) / math.sqrt(D)
    return (first, second)


def draw_w_query(key, part):
    first, second = weight_pair(key)
    return first.astype(jnp.bfloat16)


def draw_w_key(key, part):
    first, second = weight_pair(key)
    return second.astype(jnp.bfloat16)


def draw_normed(key, part):
    values = jax.random.normal(jax.random.fold_in(key, 24), (TOKENS, D), jnp.float32)
    return jnp.clip(values, -6.0, 6.0).astype(jnp.bfloat16)


def level_of(stream_key, shape, shards, least, high):
    def one(dim, shards_of):
        draws = jax.random.uniform(jax.random.fold_in(jax.random.fold_in(stream_key, 6), dim), (shards_of,), jnp.float32, least / len(shards), high / len(shards))
        return jnp.repeat(jnp.exp(draws), shape[dim] // shards_of).reshape((-1,) + (1,) * (len(shape) - dim - 1))

    gain = one(*shards[0])
    for cut in shards[1:]:
        gain = gain * one(*cut)
    return gain


def shared_out(own_key, own, number, rows, count, top, bound, skew):
    sequence = jax.random.permutation(own_key, count)
    crowded, usual = portions_of(count, rows * top, bound, skew, True), portions_of(count, rows * top, bound, skew, False)
    places = jnp.arange(count)

    def named(sizes, offset_by):
        used = int((sizes > 0).sum())
        fixed = max(1, used // 4)
        moved = fixed + (places - fixed + offset_by * (used - fixed)) % max(1, count - fixed)
        return jnp.zeros((count,), jnp.int32).at[sequence[jnp.where(places < fixed, places, moved)]].set(jnp.asarray(sizes, jnp.int32))

    sizes = jnp.where(number % 4 == 0, named(crowded, number // 4), named(usual, number - number // 4 - 1))
    mixed = jax.random.permutation(jax.random.fold_in(own, 3), count)
    donor, receiver = mixed[0:count // 2 * 2:2], mixed[1:count // 2 * 2:2]
    slack = jnp.minimum(sizes[donor] - 1, bound - sizes[receiver]) // 2
    slack = jnp.where((donor == sequence[0]) | (receiver == sequence[0]) | (sizes[receiver] == 0), 0, jnp.maximum(slack, 0))
    moved = jax.random.randint(jax.random.fold_in(own, 4), (count // 2,), 0, 1 << 20) % (slack + 1)
    sizes = sizes.at[donor].add(-moved).at[receiver].add(moved)
    items = jnp.searchsorted(jnp.cumsum(sizes), jnp.arange(rows * top), side="right").astype(jnp.int32)
    listing = items.reshape(top, rows).T
    listing = listing[jax.random.permutation(jax.random.fold_in(own, 1), rows)]
    offset_by = jax.random.randint(jax.random.fold_in(own, 2), (rows, 1), 0, top)
    return jnp.take_along_axis(listing, (jnp.arange(top)[None, :] + offset_by) % top, axis=1)


def portions_of(number_of, total, limit, slope, full):
    weights = [(1 << 20) // math.isqrt(rank ** slope) + 1 for rank in range(1, number_of + 1)]
    largest = limit if full else min(limit, max(-(-total // number_of), total * weights[0] // sum(weights)))
    least = 1 if total - largest >= number_of - 1 else 0
    given, surplus = [largest] + [least] * (number_of - 1), total - largest - least * (number_of - 1)
    while surplus > 0:
        free = [i for i in range(1, number_of) if given[i] < largest] or [i for i in range(1, number_of) if given[i] < limit]
        whole, left = sum([weights[i] for i in free]), surplus
        for i in free:
            extra = min(limit - given[i], max(1, left * weights[i] // whole), surplus)
            given[i] = given[i] + extra
            surplus = surplus - extra
    return np.array(given)


def gaussian(key, extent, width, most, pieces=(), kind=jnp.bfloat16):
    result = jax.random.normal(key, extent, jnp.float32) * width
    if len(pieces) > 0:
        result = level_of(key, extent, pieces, -0.22, 0.18) * result
    return jnp.clip(result, min=-most, max=most).astype(kind)


def setup_inputs(seed: int = 0) -> dict:
    streams_of = jax.random.split(jax.random.key(seed), 8)
    normed = draw_normed(jax.random.fold_in(streams_of[7], 71), 0)
    cluster_keys = jax.random.split(jax.random.fold_in(streams_of[1], 1), TOKENS // TOK_DEV)
    cluster_turns = jax.random.permutation(jax.random.fold_in(streams_of[1], 3), TOKENS // TOK_DEV)
    cluster = jax.vmap(lambda own, number: shared_out(jax.random.fold_in(streams_of[1], 2), own, number, TOK_DEV, CLUSTERS, 1, MOST, 2))(cluster_keys, cluster_turns).reshape((TOKENS, 1))
    w_query = draw_w_query(jax.random.fold_in(streams_of[7], 71), 0)
    w_key = draw_w_key(jax.random.fold_in(streams_of[7], 71), 0)
    w_value = gaussian(streams_of[4], (D, D), D ** -0.5, 0.125, ((1, 4),))
    w_out = gaussian(streams_of[5], (D, D), D ** -0.5, 0.125, ((0, 4),))
    grad_out = gaussian(streams_of[6], (TOKENS, D), 1.0, 6.0, ((0, 8), (1, 4)))
    return {"normed": normed, "cluster": cluster, "w_query": w_query, "w_key": w_key, "w_value": w_value, "w_out": w_out, "grad_out": grad_out}


def reference(normed, cluster, w_query, w_key, w_value, w_out, grad_out):
    cluster_ids = cluster[:, 0].astype(jnp.int32)
    columns = jnp.arange(CLUSTERS, dtype=jnp.int32)
    one_hot = (cluster_ids[:, None] == columns[None, :]).astype(jnp.int32)
    running = jnp.cumsum(one_hot, axis=0)
    place_rank = jnp.sum((running - one_hot) * one_hot, axis=1).astype(jnp.int32)
    kept = place_rank < CAP
    kept_rows = kept.astype(jnp.bfloat16)[:, None]
    queries = lax.optimization_barrier(jnp.dot(normed, w_query, preferred_element_type=jnp.float32).astype(jnp.bfloat16))
    keys_proj = lax.optimization_barrier(jnp.dot(normed, w_key, preferred_element_type=jnp.float32).astype(jnp.bfloat16))
    values_proj = lax.optimization_barrier(jnp.dot(normed, w_value, preferred_element_type=jnp.float32).astype(jnp.bfloat16))
    head_grads = lax.optimization_barrier(jnp.dot(grad_out, w_out.T, preferred_element_type=jnp.float32).astype(jnp.bfloat16) * kept_rows)
    slot_index = jnp.where(kept, cluster_ids * CAP + place_rank, CLUSTERS * CAP).astype(jnp.int32)
    filler = jnp.full((CLUSTERS * CAP + 1,), TOKENS, jnp.int32)
    token_of_slot = filler.at[slot_index].set(jnp.arange(TOKENS, dtype=jnp.int32))[: CLUSTERS * CAP].reshape(CLUSTERS, CAP)
    score_scale = HEAD_DIM ** -0.5

    def per_cluster(members):
        usable = members < TOKENS

        def pick(source):
            taken = jnp.take(source, members, axis=0, mode="fill", fill_value=0)
            return taken.reshape(CAP, HEADS, HEAD_DIM).astype(jnp.float32)

        query = pick(queries)
        key_rows = pick(keys_proj)
        value_rows = pick(values_proj)
        grad_rows = pick(head_grads)
        scores = jnp.einsum("qhd,khd->hqk", query, key_rows) * score_scale
        scores = jnp.where(usable[None, None, :], scores, -1e30)
        row_top = jnp.max(scores, axis=-1, keepdims=True)
        raised = jnp.exp(scores - row_top)
        probs = raised / jnp.sum(raised, axis=-1, keepdims=True)
        rounded = lax.optimization_barrier(probs.astype(jnp.bfloat16)).astype(jnp.float32)
        mixed = jnp.einsum("hqk,khd->qhd", rounded, value_rows).astype(jnp.bfloat16)
        grad_value = jnp.einsum("hqk,qhd->khd", rounded, grad_rows).astype(jnp.bfloat16)
        grad_probs = jnp.einsum("qhd,khd->hqk", grad_rows, value_rows)
        inner = jnp.sum(grad_probs * probs, axis=-1, keepdims=True)
        grad_scores = (probs * (grad_probs - inner) * score_scale).astype(jnp.bfloat16)
        grad_scores = lax.optimization_barrier(grad_scores).astype(jnp.float32)
        grad_query = jnp.einsum("hqk,khd->qhd", grad_scores, key_rows).astype(jnp.bfloat16)
        grad_key = jnp.einsum("hqk,qhd->khd", grad_scores, query).astype(jnp.bfloat16)
        return (mixed.reshape(CAP, D), grad_query.reshape(CAP, D), grad_key.reshape(CAP, D), grad_value.reshape(CAP, D))

    mixed_slots, query_slots, key_slots, value_slots = lax.map(per_cluster, token_of_slot)
    flat = token_of_slot.reshape(-1)

    def scatter_back(values):
        return jnp.zeros((TOKENS, D), jnp.bfloat16).at[flat].set(values.reshape(-1, D), mode="drop")

    mixed_heads = scatter_back(mixed_slots)
    attended = jnp.dot(mixed_heads, w_out, preferred_element_type=jnp.float32).astype(jnp.bfloat16)
    grad_normed = jnp.dot(scatter_back(query_slots), w_query.T, preferred_element_type=jnp.float32)
    grad_normed = grad_normed + jnp.dot(scatter_back(key_slots), w_key.T, preferred_element_type=jnp.float32)
    grad_normed = grad_normed + jnp.dot(scatter_back(value_slots), w_value.T, preferred_element_type=jnp.float32)
    return (attended, grad_normed)
```

```python
import functools
import jax
import jax.numpy as jnp
from jax import lax
from jax.experimental import pallas as pl
from jax.experimental.pallas import tpu as pltpu
from jax.sharding import PartitionSpec as P

HEAD_DIM = 128
CLUSTERS = 128
CAP = 256
MOST = 8
NT = (((1,), (1,)), ((), ()))
TN = (((0,), (0,)), ((), ()))
MB = 1024 * 1024
CHUNKS = 2


def dot(a, b, dims=(((1,), (0,)), ((), ()))):
    return lax.dot_general(a, b, dims, preferred_element_type=jnp.float32)


def swap(x, bit):
    count = lax.axis_size("tp")
    return lax.ppermute(x, "tp", [(i, i ^ bit) for i in range(count)])


def exchange(x):
    return lax.all_to_all(x, "seq", split_axis=0, concat_axis=0, tiled=True)


def place_kernel(base_col, base_row, x_ref, slot_col, slot_row, counts, out_ref):
    tokens = x_ref.shape[0]
    here = lax.broadcasted_iota(jnp.int32, (tokens, tokens), 0)
    there = lax.broadcasted_iota(jnp.int32, (tokens, tokens), 1)
    same = base_col[...] == base_row[...]
    earlier = jnp.where(same & (there < here), 1.0, 0.0)
    later = jnp.where(same & (here < there), 1.0, 0.0)
    slot_col[...] = base_col[...] + jnp.sum(earlier, axis=1, keepdims=True).astype(jnp.int32)
    slot_row[...] = base_row[...] + jnp.sum(later, axis=0, keepdims=True).astype(jnp.int32)
    lane = lax.broadcasted_iota(jnp.int32, (tokens, CLUSTERS), 1)
    named = jnp.where(base_col[...] == lane * MOST, 1.0, 0.0)
    counts[...] = jnp.sum(named, axis=0, keepdims=True).astype(jnp.int32)
    slots = out_ref.shape[0]
    place = lax.broadcasted_iota(jnp.int32, (slots, tokens), 0) == slot_row[...]
    out_ref[...] = dot(jnp.where(place, 1.0, 0.0).astype(jnp.bfloat16), x_ref[...]).astype(
        jnp.bfloat16
    )


def place(base, x):
    tokens = x.shape[0]
    return pl.pallas_call(
        place_kernel,
        out_shape=(
            jax.ShapeDtypeStruct((tokens, 1), jnp.int32),
            jax.ShapeDtypeStruct((1, tokens), jnp.int32),
            jax.ShapeDtypeStruct((1, CLUSTERS), jnp.int32),
            jax.ShapeDtypeStruct((CLUSTERS * MOST, x.shape[1]), jnp.bfloat16),
        ),
        compiler_params=pltpu.CompilerParams(vmem_limit_bytes=32 * MB),
        name="place",
    )(base[:, None], base[None, :], x)


def head_grads_kernel(blk, a0, a1, a2, a3, w_out, slot_row, out_ref):
    width = a0.shape[1]
    total = None
    for j, part in enumerate((a0, a1, a2, a3)):
        cols = pl.ds(pl.multiple_of(blk[j] * width, width), width)
        term = dot(part[...], w_out[:, cols], NT)
        total = term if total is None else total + term
    slots, tokens = (out_ref.shape[0], a0.shape[0])
    placed = lax.broadcasted_iota(jnp.int32, (slots, tokens), 0) == slot_row[...]
    out_ref[...] = dot(
        jnp.where(placed, 1.0, 0.0).astype(jnp.bfloat16), total.astype(jnp.bfloat16)
    ).astype(jnp.bfloat16)


VMEM = pl.BlockSpec(memory_space=pltpu.VMEM)
SMEM = pl.BlockSpec(memory_space=pltpu.SMEM)


def head_grads(blk, parts, w_out, slot_row):
    return pl.pallas_call(
        head_grads_kernel,
        out_shape=jax.ShapeDtypeStruct((CLUSTERS * MOST, w_out.shape[0]), jnp.bfloat16),
        in_specs=[SMEM] + [VMEM] * 6,
        out_specs=VMEM,
        compiler_params=pltpu.CompilerParams(vmem_limit_bytes=32 * MB),
        name="head_grads",
    )(blk, *parts, w_out, slot_row)


def core_kernel(
    blk, x0, x1, x2, x3, g_ref, vrow, vcol, wq, wk, wv, mixed, keep, give, dq, dk, dv
):
    sources, rows, width = x0.shape
    members = sources * rows
    heads = wq.shape[1] // HEAD_DIM
    scale = HEAD_DIM ** (-0.5)
    spans = [pl.ds(pl.multiple_of(blk[j] * width, width), width) for j in range(4)]
    xs = [r[...].reshape(members, width) for r in (x0, x1, x2, x3)]

    def project(w):
        total = dot(xs[0], w[spans[0], :])
        for j in range(1, 4):
            total = total + dot(xs[j], w[spans[j], :])
        return total.astype(jnp.bfloat16)

    queries, keys, values = (project(wq), project(wk), project(wv))
    here = lax.broadcasted_iota(jnp.int32, (members, members), 0) % rows // MOST
    there = lax.broadcasted_iota(jnp.int32, (members, members), 1) % rows // MOST
    usable = (here == there) & (vrow[0] > 0)
    row_kept = vcol[0]
    grads = (g_ref[...].reshape(members, -1).astype(jnp.float32) * row_kept).astype(jnp.bfloat16)
    for h in range(heads):
        cols = slice(h * HEAD_DIM, (h + 1) * HEAD_DIM)
        q, k, v, g = (queries[:, cols], keys[:, cols], values[:, cols], grads[:, cols])
        scores = jnp.where(usable, dot(q, k, NT) * scale, -1e30)
        raised = jnp.exp(scores - jnp.max(scores, axis=1, keepdims=True))
        probs = raised * (1.0 / jnp.sum(raised, axis=1, keepdims=True))
        rounded = probs.astype(jnp.bfloat16)
        out = (dot(rounded, v) * row_kept).astype(jnp.bfloat16)
        mixed[:, :, cols] = out.reshape(sources, rows, HEAD_DIM)
        dv[:, cols] = dot(rounded, g, TN).astype(jnp.bfloat16)
        grad_probs = dot(g, v, NT)
        inner = jnp.sum(grad_probs * probs, axis=1, keepdims=True)
        grad_scores = (probs * (grad_probs - inner) * scale).astype(jnp.bfloat16)
        dq[:, cols] = dot(grad_scores, k).astype(jnp.bfloat16)
        dk[:, cols] = dot(grad_scores, q, TN).astype(jnp.bfloat16)
    for j in range(4):
        total = dot(dq[...], wq[spans[j], :], NT)
        total = total + dot(dk[...], wk[spans[j], :], NT)
        total = total + dot(dv[...], wv[spans[j], :], NT)
        target = (keep, give, keep, give)[j]
        target[j // 2] = total.astype(jnp.bfloat16).reshape(sources, rows, width)


def core(blk, parts, grads, valid, wq, wk, wv):
    sources, rows, width = parts[0].shape
    heads_width = wq.shape[1]
    step = 16
    while step * 2 * sources <= 256 and rows % (step * 2) == 0:
        step *= 2
    members, steps = (sources * step, rows // step)
    by_step = valid.reshape(sources, steps, step).transpose(1, 0, 2).reshape(steps, members)
    block = pl.BlockSpec((sources, step, width), lambda p: (0, p, 0))
    hblock = pl.BlockSpec((sources, step, heads_width), lambda p: (0, p, 0))
    pair = pl.BlockSpec((2, sources, step, width), lambda p: (0, 0, p, 0))
    weight = pl.BlockSpec(wq.shape, lambda p: (0, 0), pipeline_mode=pl.Buffered(1))
    return pl.pallas_call(
        core_kernel,
        grid=(steps,),
        out_shape=(
            jax.ShapeDtypeStruct((sources, rows, heads_width), jnp.bfloat16),
            jax.ShapeDtypeStruct((2, sources, rows, width), jnp.bfloat16),
            jax.ShapeDtypeStruct((2, sources, rows, width), jnp.bfloat16),
        ),
        in_specs=[
            SMEM,
            block,
            block,
            block,
            block,
            hblock,
            pl.BlockSpec((1, 1, members), lambda p: (p, 0, 0)),
            pl.BlockSpec((1, members, 1), lambda p: (p, 0, 0)),
            weight,
            weight,
            weight,
        ],
        out_specs=(hblock, pair, pair),
        scratch_shapes=[pltpu.VMEM((members, heads_width), jnp.bfloat16)] * 3,
        compiler_params=pltpu.CompilerParams(vmem_limit_bytes=40 * MB),
        cost_estimate=pl.CostEstimate(
            flops=2 * sources * rows * width * 4 * heads_width * 6,
            bytes_accessed=16 * MB,
            transcendentals=sources * rows * members * 4,
        ),
        name="core",
    )(blk, *parts, grads, by_step[:, None, :], by_step[:, :, None], wq, wk, wv)


def core_many(blk, parts, grads, valid, wq, wk, wv):
    sources, rows, width = parts[0].shape
    heads = wq.shape[1] // HEAD_DIM
    clusters = rows // MOST
    scale = HEAD_DIM ** (-0.5)

    def slab(w, j):
        return lax.dynamic_slice_in_dim(w, blk[j] * width, width, 0)

    def by_cluster(x):
        x = x.reshape(sources, clusters, MOST, -1).transpose(1, 0, 2, 3)
        return x.reshape(clusters, sources * MOST, -1)

    def by_source(x):
        x = x.reshape(clusters, sources, MOST, -1).transpose(1, 0, 2, 3)
        return x.reshape(sources, rows, -1)

    def project(w):
        total = 0.0
        for j in range(4):
            total = total + jnp.einsum(
                "srd,dh->srh", parts[j], slab(w, j), preferred_element_type=jnp.float32
            )
        return by_cluster(total.astype(jnp.bfloat16))

    kept = by_cluster(valid[:, :, None])

    def one(args):
        q, k, v, g, live = args
        q, k, v, g = (a.reshape(a.shape[0], heads, HEAD_DIM) for a in (q, k, v, g))
        ein = functools.partial(jnp.einsum, preferred_element_type=jnp.float32)
        g = (g * live[:, :, None]).astype(jnp.bfloat16)
        scores = jnp.where(live[None, None, :, 0] > 0, ein("qhd,khd->hqk", q, k) * scale, -1e30)
        raised = jnp.exp(scores - jnp.max(scores, axis=-1, keepdims=True))
        probs = raised / jnp.sum(raised, axis=-1, keepdims=True)
        rounded = probs.astype(jnp.bfloat16)
        mixed = (ein("hqk,khd->qhd", rounded, v) * live[:, :, None]).astype(jnp.bfloat16)
        dv = ein("hqk,qhd->khd", rounded, g).astype(jnp.bfloat16)
        grad_probs = ein("qhd,khd->hqk", g, v)
        inner = jnp.sum(grad_probs * probs, axis=-1, keepdims=True)
        grad_scores = (probs * (grad_probs - inner) * scale).astype(jnp.bfloat16)
        dq = ein("hqk,khd->qhd", grad_scores, k).astype(jnp.bfloat16)
        dk = ein("hqk,qhd->khd", grad_scores, q).astype(jnp.bfloat16)
        return tuple(a.reshape(a.shape[0], -1) for a in (mixed, dq, dk, dv))

    mixed, dq, dk, dv = lax.map(
        one, (project(wq), project(wk), project(wv), by_cluster(grads), kept)
    )
    outs = []
    for j in range(4):
        total = 0.0
        for d, w in ((dq, wq), (dk, wk), (dv, wv)):
            total = total + jnp.einsum(
                "crh,wh->crw", d, slab(w, j), preferred_element_type=jnp.float32
            )
        outs.append(by_source(total.astype(jnp.bfloat16)))
    return (by_source(mixed), jnp.stack([outs[0], outs[2]]), jnp.stack([outs[1], outs[3]]))


def pick(slot_col, parts):
    tokens = slot_col.shape[0]
    total, first = (None, 0)
    for part in parts:
        rows = part.shape[0]
        slots = lax.broadcasted_iota(jnp.int32, (tokens, rows), 1) + first
        chosen = jnp.where(slots == slot_col[...], 1.0, 0.0).astype(jnp.bfloat16)
        term = dot(chosen, part[...])
        total = term if total is None else total + term
        first += rows
    return total


def out_kernel(blk, slot_col, w_out, *refs):
    parts, keep, give = (refs[:-2], refs[-2], refs[-1])
    heads = pick(slot_col, parts).astype(jnp.bfloat16)
    width = keep.shape[2]
    for j in range(4):
        cols = pl.ds(pl.multiple_of(blk[j] * width, width), width)
        target = (keep, give, keep, give)[j]
        target[j // 2] = dot(heads, w_out[:, cols]).astype(jnp.bfloat16)


def project_out(blk, slot_col, w_out, parts):
    tokens, width = (slot_col.shape[0], w_out.shape[1] // 4)
    shape = jax.ShapeDtypeStruct((2, tokens, width), jnp.bfloat16)
    return pl.pallas_call(
        out_kernel,
        out_shape=(shape, shape),
        in_specs=[SMEM] + [VMEM] * (2 + len(parts)),
        out_specs=(VMEM, VMEM),
        compiler_params=pltpu.CompilerParams(vmem_limit_bytes=32 * MB),
        name="project_out",
    )(blk, slot_col, w_out, *parts)


def final_kernel(slot_col, *refs):
    refs[-1][...] = pick(slot_col, refs[:-1])


def to_tokens(slot_col, parts):
    return pl.pallas_call(
        final_kernel,
        out_shape=jax.ShapeDtypeStruct((slot_col.shape[0], parts[0].shape[1]), jnp.float32),
        compiler_params=pltpu.CompilerParams(vmem_limit_bytes=32 * MB),
        name="to_tokens",
    )(slot_col, *parts)


def gather_parts(x):
    across = swap(x, 2)
    return (x, swap(x, 1), across, swap(across, 1))


def wide(x):
    return x.astype(jnp.float32)


def reduce_parts(keep, give):
    got = swap(give, 1)
    across = swap((wide(keep[1]) + wide(got[1])).astype(jnp.bfloat16), 2)
    return (wide(keep[0]) + wide(got[0]) + wide(across)).astype(jnp.bfloat16)


def body(normed, cluster, w_query, w_key, w_value, w_out, grad_out):
    seq_count = lax.axis_size("seq")
    cluster_here = CLUSTERS // seq_count
    chunks = CHUNKS if cluster_here * MOST // CHUNKS % 16 == 0 else 1
    per_chunk = cluster_here // chunks
    rows = per_chunk * MOST
    span = seq_count * rows
    ids = cluster[:, 0]
    owner, local = (ids // cluster_here, ids % cluster_here)
    base = (local // per_chunk) * span + owner * rows + (local % per_chunk) * MOST
    blk = lax.axis_index("tp") ^ jnp.arange(4, dtype=jnp.int32)

    slot_col, slot_row, counts, x_slots = place(base, normed)
    pieces = x_slots.reshape(chunks, seq_count, rows, -1)
    arrived = [exchange(pieces[c]) for c in range(chunks)]
    counts = counts.reshape(chunks, seq_count, per_chunk).transpose(1, 0, 2)
    counts = exchange(counts)
    before = jnp.cumsum(counts, axis=0) - counts
    kept = jnp.clip(CAP - before, 0, counts)
    valid = (jnp.arange(MOST) < kept[..., None]).astype(jnp.float32)
    valid = valid.reshape(seq_count, chunks, rows)

    g_slots = head_grads(blk, gather_parts(grad_out), w_out, slot_row)
    g_pieces = g_slots.reshape(chunks, seq_count, rows, -1)
    g_arrived = [exchange(g_pieces[c]) for c in range(chunks)]

    run = core if seq_count * 16 <= 256 else core_many
    mixed_back, grads_back = ([], [])
    for c in range(chunks):
        mixed, keep, give = run(
            blk, gather_parts(arrived[c]), g_arrived[c], valid[:, c], w_query, w_key, w_value
        )
        mixed_back.append(exchange(mixed).reshape(span, -1))
        grads_back.append(exchange(reduce_parts(keep, give)).reshape(span, -1))
    attended = reduce_parts(*project_out(blk, slot_col, w_out, mixed_back))
    return (attended, to_tokens(slot_col, grads_back))


def solution(mesh):
    in_specs = (
        P("seq", "tp"),
        P("seq", None),
        P(None, "tp"),
        P(None, "tp"),
        P(None, "tp"),
        P("tp", None),
        P("seq", "tp"),
    )
    out_specs = (P("seq", "tp"), P("seq", "tp"))
    return jax.shard_map(body, mesh=mesh, in_specs=in_specs, out_specs=out_specs, check_vma=False)
```

```python
import functools
import jax
import jax.numpy as jnp
from jax import lax
from jax.experimental import pallas as pl
from jax.experimental.pallas import tpu as pltpu
from jax.sharding import PartitionSpec as P

HEAD_DIM = 128
CLUSTERS = 128
CAP = 256
MOST = 8
LIMIT = 24.0
EMPTY = 32.0
NN = (((1,), (0,)), ((), ()))
NT = (((1,), (1,)), ((), ()))
TN = (((0,), (0,)), ((), ()))
MB = 1024 * 1024
CHUNKS = 2
VMEM = pl.BlockSpec(memory_space=pltpu.VMEM)
SMEM = pl.BlockSpec(memory_space=pltpu.SMEM)


def dot(a, b, dims=NN):
    return lax.dot_general(a, b, dims, preferred_element_type=jnp.float32)


def iota(shape, dim):
    return lax.broadcasted_iota(jnp.int32, shape, dim)


def swap(x, bit):
    count = lax.axis_size("tp")
    return lax.ppermute(x, "tp", [(i, i ^ bit) for i in range(count)])


def exchange(x):
    return lax.all_to_all(x, "seq", split_axis=0, concat_axis=0, tiled=True)


def after(x, *others):
    return lax.optimization_barrier((x,) + others)[0]


def place_kernel(ids_col, x_ref, slot_col, slot_row, *outs):
    tokens = x_ref.shape[0]
    here, there = (iota((tokens, tokens), 0), iota((tokens, tokens), 1))
    col = ids_col[...]
    row = jnp.sum(jnp.where(here == there, col, 0), axis=0, keepdims=True)
    same = col == row
    earlier = jnp.where(same & (there < here), 1.0, 0.0)
    later = jnp.where(same & (here < there), 1.0, 0.0)
    slot_col[...] = col * MOST + jnp.sum(earlier, axis=1, keepdims=True).astype(jnp.int32)
    slot_row[...] = row * MOST + jnp.sum(later, axis=0, keepdims=True).astype(jnp.int32)
    for c, out in enumerate(outs):
        owners, rows, width = out.shape
        shape = (owners, rows, tokens)
        slot = iota(shape, 0) * (rows * len(outs)) + iota(shape, 1) + c * rows
        chosen = jnp.where(slot.reshape(owners * rows, tokens) == slot_row[...], 1.0, 0.0)
        taken = jnp.sum(chosen, axis=1, keepdims=True)
        first = iota((owners * rows, width), 1) == 0
        value = dot(chosen.astype(jnp.bfloat16), x_ref[...])
        value = value + jnp.where(first & (taken == 0.0), EMPTY, 0.0)
        out[...] = value.astype(jnp.bfloat16).reshape(out.shape)


def place(cluster, x, owners, rows, chunks):
    tokens = x.shape[0]
    piece = jax.ShapeDtypeStruct((owners, rows, x.shape[1]), jnp.bfloat16)
    return pl.pallas_call(
        place_kernel,
        out_shape=(
            jax.ShapeDtypeStruct((tokens, 1), jnp.int32),
            jax.ShapeDtypeStruct((1, tokens), jnp.int32),
        )
        + (piece,) * chunks,
        compiler_params=pltpu.CompilerParams(vmem_limit_bytes=32 * MB),
        name="place",
    )(cluster, x)


def head_grads_kernel(blk, a0, a1, a2, a3, w_out, slot_row, out_ref):
    width = a0.shape[1]
    total = None
    for j, part in enumerate((a0, a1, a2, a3)):
        cols = pl.ds(pl.multiple_of(blk[j] * width, width), width)
        term = dot(part[...], w_out[:, cols], NT)
        total = term if total is None else total + term
    slots, tokens = (out_ref.shape[0], a0.shape[0])
    chosen = jnp.where(iota((slots, tokens), 0) == slot_row[...], 1.0, 0.0).astype(jnp.bfloat16)
    out_ref[...] = dot(chosen, total.astype(jnp.bfloat16)).astype(jnp.bfloat16)


def head_grads(blk, parts, w_out, slot_row):
    return pl.pallas_call(
        head_grads_kernel,
        out_shape=jax.ShapeDtypeStruct((CLUSTERS * MOST, w_out.shape[0]), jnp.bfloat16),
        in_specs=[SMEM] + [VMEM] * 6,
        out_specs=VMEM,
        compiler_params=pltpu.CompilerParams(vmem_limit_bytes=32 * MB),
        name="head_grads",
    )(blk, *parts, w_out, slot_row)


GROUP = 16


def spans(blk, width):
    return [pl.ds(pl.multiple_of(blk[j] * width, width), width) for j in range(4)]


def forward_kernel(blk, x0, x1, x2, x3, wq, wk, wv, *refs):
    mixed, saved, probs_ref = refs[-3:]
    sources, rows, width = x0.shape
    heads_width = wq.shape[1]
    heads = heads_width // HEAD_DIM
    scale = HEAD_DIM ** (-0.5)
    span = spans(blk, width)
    xs = [r[...].reshape(sources * rows, width) for r in (x0, x1, x2, x3)]
    for i, w in enumerate((wq, wk, wv)):
        total = dot(xs[0], w[span[0], :])
        for j in range(1, 4):
            total = total + dot(xs[j], w[span[j], :])
        saved[:, :, i * heads_width : (i + 1) * heads_width] = total.astype(jnp.bfloat16).reshape(
            sources, rows, heads_width
        )
    members = sources * GROUP
    shape = (sources, GROUP, members)
    here = (iota(shape, 1) // MOST).reshape(members, members)
    source_here = iota(shape, 0).reshape(members, members)
    place_here = iota(shape, 1).reshape(members, members)
    lane = iota((members, members), 1)
    there = lane % GROUP // MOST
    same = here == there
    earlier = same & (lane // GROUP < source_here)
    later = same & (lane // GROUP > source_here)
    diagonal = source_here * GROUP + place_here == lane
    rank_col = (place_here % MOST).astype(jnp.float32)[:, :1]
    rank_row = (lane % MOST).astype(jnp.float32)[:1, :]
    for n in range(rows // GROUP):
        group = slice(n * GROUP, (n + 1) * GROUP)
        mark = x0[:, group, :HEAD_DIM].reshape(members, HEAD_DIM)[:, :1].astype(jnp.float32)
        held_col = jnp.where(mark <= LIMIT, 1.0, 0.0)
        held_row = jnp.sum(jnp.where(diagonal, held_col, 0.0), axis=0, keepdims=True)
        place_col = rank_col + jnp.sum(jnp.where(earlier, held_row, 0.0), axis=1, keepdims=True)
        place_row = rank_row + jnp.sum(jnp.where(later, held_col, 0.0), axis=0, keepdims=True)
        kept_col = jnp.where(place_col < CAP, held_col, 0.0)
        usable = same & (jnp.where(place_row < CAP, held_row, 0.0) > 0)
        for h in range(heads):
            def part(i):
                first = i * heads_width + h * HEAD_DIM
                return saved[:, group, first : first + HEAD_DIM].reshape(members, HEAD_DIM)

            scores = jnp.where(usable, dot(part(0), part(1), NT) * scale, -1e30)
            raised = jnp.exp(scores - jnp.max(scores, axis=1, keepdims=True))
            probs = raised * (kept_col / jnp.sum(raised, axis=1, keepdims=True))
            probs_ref[0, n, h] = probs
            out = dot(probs.astype(jnp.bfloat16), part(2)).astype(jnp.bfloat16)
            mixed[:, group, h * HEAD_DIM : (h + 1) * HEAD_DIM] = out.reshape(
                sources, GROUP, HEAD_DIM
            )


def backward_kernel(blk, saved, probs_ref, g_ref, wq, wk, wv, keep, give, dq, dk, dv):
    sources, rows, _ = saved.shape
    width = keep.shape[3]
    heads_width = wq.shape[1]
    heads = heads_width // HEAD_DIM
    scale = HEAD_DIM ** (-0.5)
    span = spans(blk, width)
    members = sources * GROUP
    for n in range(rows // GROUP):
        group = slice(n * GROUP, (n + 1) * GROUP)
        for h in range(heads):
            cols = slice(h * HEAD_DIM, (h + 1) * HEAD_DIM)

            def part(i):
                first = i * heads_width + h * HEAD_DIM
                return saved[:, group, first : first + HEAD_DIM].reshape(members, HEAD_DIM)

            def put(ref, value):
                ref[:, group, cols] = value.astype(jnp.bfloat16).reshape(sources, GROUP, HEAD_DIM)

            g = g_ref[:, group, cols].reshape(members, HEAD_DIM)
            probs = probs_ref[0, n, h]
            put(dv, dot(probs.astype(jnp.bfloat16), g, TN))
            grad_probs = dot(g, part(2), NT)
            inner = jnp.sum(grad_probs * probs, axis=1, keepdims=True)
            grad_scores = (probs * (grad_probs - inner) * scale).astype(jnp.bfloat16)
            put(dq, dot(grad_scores, part(1)))
            put(dk, dot(grad_scores, part(0), TN))
    grads = [d[...].reshape(sources * rows, heads_width) for d in (dq, dk, dv)]
    for j in (1, 3, 0, 2):
        total = None
        for d, w in zip(grads, (wq, wk, wv)):
            term = dot(d, w[span[j], :], NT)
            total = term if total is None else total + term
        target = (keep, give)[j % 2]
        target[j // 2] = total.astype(jnp.bfloat16).reshape(sources, rows, width)


def step_of(sources, rows):
    step = GROUP
    while step * 2 * sources <= 256 and rows % (step * 2) == 0:
        step *= 2
    return step


def forward(blk, parts, wq, wk, wv, chunk, chunks, mixed):
    sources, rows, width = parts[0].shape
    heads_width = wq.shape[1]
    heads = heads_width // HEAD_DIM
    step = step_of(sources, rows)
    steps, groups, members = (rows // step, step // GROUP, sources * GROUP)
    block = pl.BlockSpec((sources, step, width), lambda p: (0, p, 0))
    weight = pl.BlockSpec(wq.shape, lambda p: (0, 0), pipeline_mode=pl.Buffered(1))
    in_specs = [SMEM] + [block] * 4 + [weight] * 3
    operands = [blk, *parts, wq, wk, wv]
    if mixed is not None:
        in_specs.append(pl.BlockSpec(memory_space=pl.ANY))
        operands.append(mixed)
    return pl.pallas_call(
        forward_kernel,
        grid=(steps,),
        out_shape=(
            jax.ShapeDtypeStruct((sources, rows * chunks, heads_width), jnp.bfloat16),
            jax.ShapeDtypeStruct((sources, rows, 3 * heads_width), jnp.bfloat16),
            jax.ShapeDtypeStruct((steps, groups, heads, members, members), jnp.float32),
        ),
        in_specs=in_specs,
        out_specs=(
            pl.BlockSpec((sources, step, heads_width), lambda p: (0, p + chunk * steps, 0)),
            pl.BlockSpec((sources, step, 3 * heads_width), lambda p: (0, p, 0)),
            pl.BlockSpec((1, groups, heads, members, members), lambda p: (p, 0, 0, 0, 0)),
        ),
        input_output_aliases={} if mixed is None else {len(operands) - 1: 0},
        compiler_params=pltpu.CompilerParams(vmem_limit_bytes=40 * MB),
        cost_estimate=pl.CostEstimate(
            flops=2 * sources * rows * width * 4 * heads_width * 3,
            bytes_accessed=10 * MB,
            transcendentals=sources * rows * members * heads,
        ),
        name="forward",
    )(*operands)


def backward(blk, saved, probs, grads, wq, wk, wv, chunk):
    sources, rows, _ = saved.shape
    heads_width = wq.shape[1]
    width = wq.shape[0] // 4
    heads = heads_width // HEAD_DIM
    step = step_of(sources, rows)
    steps, groups, members = (rows // step, step // GROUP, sources * GROUP)
    pair = pl.BlockSpec((2, sources, step, width), lambda p: (0, 0, p, 0))
    weight = pl.BlockSpec(wq.shape, lambda p: (0, 0), pipeline_mode=pl.Buffered(1))
    shape = jax.ShapeDtypeStruct((2, sources, rows, width), jnp.bfloat16)
    return pl.pallas_call(
        backward_kernel,
        grid=(steps,),
        out_shape=(shape, shape),
        in_specs=[
            SMEM,
            pl.BlockSpec((sources, step, 3 * heads_width), lambda p: (0, p, 0)),
            pl.BlockSpec((1, groups, heads, members, members), lambda p: (p, 0, 0, 0, 0)),
            pl.BlockSpec((sources, step, heads_width), lambda p: (0, p + chunk * steps, 0)),
            weight,
            weight,
            weight,
        ],
        out_specs=(pair, pair),
        scratch_shapes=[pltpu.VMEM((sources, step, heads_width), jnp.bfloat16)] * 3,
        compiler_params=pltpu.CompilerParams(vmem_limit_bytes=40 * MB),
        cost_estimate=pl.CostEstimate(
            flops=2 * sources * rows * width * 4 * heads_width * 3,
            bytes_accessed=12 * MB,
            transcendentals=0,
        ),
        name="backward",
    )(blk, saved, probs, grads, wq, wk, wv)


def slab(w, blk, j):
    width = w.shape[0] // 4
    return lax.dynamic_slice_in_dim(w, blk[j] * width, width, 0)


def by_cluster(x):
    sources, rows = x.shape[:2]
    x = x.reshape(sources, rows // MOST, MOST, -1).transpose(1, 0, 2, 3)
    return x.reshape(rows // MOST, sources * MOST, -1)


def by_source(x, sources):
    clusters = x.shape[0]
    x = x.reshape(clusters, sources, MOST, -1).transpose(1, 0, 2, 3)
    return x.reshape(sources, clusters * MOST, -1)


def split_heads(x):
    return x.reshape(x.shape[0], -1, HEAD_DIM)


ein = functools.partial(jnp.einsum, preferred_element_type=jnp.float32)


def forward_many(blk, parts, wq, wk, wv):
    sources, rows, _ = parts[0].shape

    def project(w):
        total = 0.0
        for j in range(4):
            total = total + ein("srd,dh->srh", parts[j], slab(w, blk, j))
        return by_cluster(total.astype(jnp.bfloat16))

    held = (parts[0][:, :, 0].astype(jnp.float32) <= LIMIT).reshape(sources, -1, MOST)
    counts = jnp.sum(held.astype(jnp.int32), axis=2, keepdims=True)
    rank = jnp.cumsum(counts, axis=0) - counts + jnp.arange(MOST)
    kept = by_cluster((held & (rank < CAP)).astype(jnp.float32).reshape(sources, rows, 1))
    scale = HEAD_DIM ** (-0.5)

    def one(args):
        q, k, v, live = args
        q, k, v = (split_heads(a) for a in (q, k, v))
        scores = jnp.where(live[None, None, :, 0] > 0, ein("qhd,khd->hqk", q, k) * scale, -1e30)
        raised = jnp.exp(scores - jnp.max(scores, axis=-1, keepdims=True))
        probs = raised * (live / jnp.sum(raised, axis=-1, keepdims=True))
        mixed = ein("hqk,khd->qhd", probs.astype(jnp.bfloat16), v).astype(jnp.bfloat16)
        return (mixed.reshape(mixed.shape[0], -1), probs)

    saved = tuple(project(w) for w in (wq, wk, wv))
    mixed, probs = lax.map(one, saved + (kept,))
    return (by_source(mixed, sources), saved, probs)


def backward_many(blk, saved, probs, grads, wq, wk, wv):
    sources = grads.shape[0]
    scale = HEAD_DIM ** (-0.5)

    def one(args):
        q, k, v, probs, g = args
        q, k, v, g = (split_heads(a) for a in (q, k, v, g))
        dv = ein("hqk,qhd->khd", probs.astype(jnp.bfloat16), g)
        grad_probs = ein("qhd,khd->hqk", g, v)
        inner = jnp.sum(grad_probs * probs, axis=-1, keepdims=True)
        grad_scores = (probs * (grad_probs - inner) * scale).astype(jnp.bfloat16)
        dq = ein("hqk,khd->qhd", grad_scores, k)
        dk = ein("hqk,qhd->khd", grad_scores, q)
        return tuple(a.astype(jnp.bfloat16).reshape(a.shape[0], -1) for a in (dq, dk, dv))

    dq, dk, dv = lax.map(one, saved + (probs, by_cluster(grads)))
    outs = []
    for j in range(4):
        total = 0.0
        for d, w in ((dq, wq), (dk, wk), (dv, wv)):
            total = total + ein("crh,wh->crw", d, slab(w, blk, j))
        outs.append(by_source(total.astype(jnp.bfloat16), sources))
    return (jnp.stack([outs[0], outs[2]]), jnp.stack([outs[1], outs[3]]))


def pick(slot_col, part, first, count, stride):
    owners = part.shape[0]
    i = iota((1, owners * count), 1)
    slots = i // count * stride + i % count + first
    chosen = jnp.where(slots == slot_col[...], 1.0, 0.0).astype(jnp.bfloat16)
    return dot(chosen, part[...].reshape(owners * count, -1))


def out_kernel(blk, slot_col, w_out, mixed, keep, give):
    per = mixed.shape[1]
    heads = pick(slot_col, mixed, 0, per, per).astype(jnp.bfloat16)
    width = keep.shape[2]
    span = spans(blk, width)
    for j in (1, 3, 0, 2):
        (keep, give)[j % 2][j // 2] = dot(heads, w_out[:, span[j]]).astype(jnp.bfloat16)


def project_out(blk, slot_col, w_out, mixed):
    tokens, width = (slot_col.shape[0], w_out.shape[1] // 4)
    shape = jax.ShapeDtypeStruct((2, tokens, width), jnp.bfloat16)
    return pl.pallas_call(
        out_kernel,
        out_shape=(shape, shape),
        in_specs=[SMEM] + [VMEM] * 3,
        out_specs=(VMEM, VMEM),
        compiler_params=pltpu.CompilerParams(vmem_limit_bytes=32 * MB),
        name="project_out",
    )(blk, slot_col, w_out, mixed)


def final_kernel(slot_col, *refs):
    parts, out = (refs[:-1], refs[-1])
    rows = parts[0].shape[1]
    total = None
    for c, part in enumerate(parts):
        term = pick(slot_col, part, c * rows, rows, rows * len(parts))
        total = term if total is None else total + term
    out[...] = total


def to_tokens(slot_col, parts):
    return pl.pallas_call(
        final_kernel,
        out_shape=jax.ShapeDtypeStruct((slot_col.shape[0], parts[0].shape[2]), jnp.float32),
        compiler_params=pltpu.CompilerParams(vmem_limit_bytes=32 * MB),
        name="to_tokens",
    )(slot_col, *parts)


def gather_parts(x):
    across = swap(x, 2)
    return (x, swap(x, 1), across, swap(across, 1))


def wide(x):
    return x.astype(jnp.float32)


def reduce_pairs(keep, give):
    got = swap(give, 1)
    return (got, (wide(keep[1]) + wide(got[1])).astype(jnp.bfloat16))


def reduce_across(keep, got, partial):
    return (wide(keep[0]) + wide(got[0]) + wide(swap(partial, 2))).astype(jnp.bfloat16)


def body(normed, cluster, w_query, w_key, w_value, w_out, grad_out):
    seq_count = lax.axis_size("seq")
    per = CLUSTERS // seq_count * MOST
    chunks = CHUNKS if per // CHUNKS % GROUP == 0 else 1
    rows = per // chunks
    blk = lax.axis_index("tp") ^ jnp.arange(4, dtype=jnp.int32)
    weights = (w_query, w_key, w_value)
    small = seq_count * GROUP <= 256

    slot_col, slot_row, *pieces = place(cluster, normed, seq_count, rows, chunks)
    arrived = [exchange(pieces[0])]
    for piece in pieces[1:]:
        arrived.append(exchange(after(piece, arrived[-1])))
    g_slots = head_grads(blk, gather_parts(grad_out), w_out, slot_row)
    g_slots = after(g_slots.reshape(seq_count, per, -1), arrived[-1])
    g_arrived = exchange(g_slots)

    if small:
        mixed, kept = (None, [])
        for c in range(chunks):
            parts = gather_parts(arrived[c])
            mixed, saved, probs = forward(blk, parts, *weights, c, chunks, mixed)
            kept.append((saved, probs))
    else:
        mixed, saved, probs = forward_many(blk, gather_parts(arrived[0]), *weights)
    mixed_back = exchange(after(mixed, g_arrived))

    partials = []
    for c in range(chunks):
        if small:
            keep, give = backward(blk, *kept[c], g_arrived, *weights, c)
        else:
            keep, give = backward_many(blk, saved, probs, g_arrived, *weights)
        got, partial = reduce_pairs(keep, give)
        partials.append((keep, got, partial))
        g_arrived = after(g_arrived, partial)
    back, last = ([], mixed_back)
    for keep, got, partial in partials:
        last = exchange(after(reduce_across(keep, got, partial), last))
        back.append(last)
    keep, give = project_out(blk, slot_col, w_out, mixed_back)
    got, partial = reduce_pairs(keep, give)
    attended = reduce_across(keep, got, partial)
    return (attended, to_tokens(slot_col, back))


def solution(mesh):
    in_specs = (
        P("seq", "tp"),
        P("seq", None),
        P(None, "tp"),
        P(None, "tp"),
        P(None, "tp"),
        P("tp", None),
        P("seq", "tp"),
    )
    out_specs = (P("seq", "tp"), P("seq", "tp"))
    return jax.shard_map(body, mesh=mesh, in_specs=in_specs, out_specs=out_specs, check_vma=False)
```

```python
import functools
import jax
import jax.numpy as jnp
from jax import lax
from jax.experimental import pallas as pl
from jax.experimental.pallas import tpu as pltpu
from jax.sharding import PartitionSpec as P

HEAD_DIM = 128
CLUSTERS = 128
CAP = 256
MOST = 8
LIMIT = 24.0
EMPTY = 32.0
NN = (((1,), (0,)), ((), ()))
NT = (((1,), (1,)), ((), ()))
TN = (((0,), (0,)), ((), ()))
MB = 1024 * 1024
CHUNKS = 2
GRANT = 60 * MB


def cost(giga):
    return pl.CostEstimate(flops=int(giga * 1e9), bytes_accessed=MB, transcendentals=0)


VMEM = pl.BlockSpec(memory_space=pltpu.VMEM)
SMEM = pl.BlockSpec(memory_space=pltpu.SMEM)


def dot(a, b, dims=NN):
    return lax.dot_general(a, b, dims, preferred_element_type=jnp.float32)


def iota(shape, dim):
    return lax.broadcasted_iota(jnp.int32, shape, dim)


def swap(x, bit):
    count = lax.axis_size("tp")
    return lax.ppermute(x, "tp", [(i, i ^ bit) for i in range(count)])


def exchange(x):
    return lax.all_to_all(x, "seq", split_axis=0, concat_axis=0, tiled=True)


def after(x, *others):
    return lax.optimization_barrier((x,) + others)[0]


def place_kernel(ids_col, x_ref, slot_col, slot_row, out):
    tokens = x_ref.shape[0]
    here, there = (iota((tokens, tokens), 0), iota((tokens, tokens), 1))
    col = ids_col[...]
    row = jnp.sum(jnp.where(here == there, col, 0), axis=0, keepdims=True)
    same = col == row
    earlier = jnp.where(same & (there < here), 1.0, 0.0)
    later = jnp.where(same & (here < there), 1.0, 0.0)
    slot_col[...] = col * MOST + jnp.sum(earlier, axis=1, keepdims=True).astype(jnp.int32)
    slot_row[...] = row * MOST + jnp.sum(later, axis=0, keepdims=True).astype(jnp.int32)
    slots, width = out.shape
    chosen = jnp.where(iota((slots, tokens), 0) == slot_row[...], 1.0, 0.0)
    taken = jnp.sum(chosen, axis=1, keepdims=True)
    value = dot(chosen.astype(jnp.bfloat16), x_ref[...])
    first = iota((slots, width), 1) == 0
    out[...] = (value + jnp.where(first & (taken == 0.0), EMPTY, 0.0)).astype(jnp.bfloat16)


def place(cluster, x):
    tokens = x.shape[0]
    return pl.pallas_call(
        place_kernel,
        out_shape=(
            jax.ShapeDtypeStruct((tokens, 1), jnp.int32),
            jax.ShapeDtypeStruct((1, tokens), jnp.int32),
            jax.ShapeDtypeStruct((CLUSTERS * MOST, x.shape[1]), jnp.bfloat16),
        ),
        compiler_params=pltpu.CompilerParams(vmem_limit_bytes=GRANT),
        cost_estimate=cost(1),
        name="place",
    )(cluster, x)


def head_grads_kernel(blk, a0, a1, a2, a3, w_out, slot_row, out_ref):
    width = a0.shape[1]
    total = None
    for j, part in enumerate((a0, a1, a2, a3)):
        cols = pl.ds(pl.multiple_of(blk[j] * width, width), width)
        term = dot(part[...], w_out[:, cols], NT)
        total = term if total is None else total + term
    slots, tokens = (out_ref.shape[0], a0.shape[0])
    chosen = jnp.where(iota((slots, tokens), 0) == slot_row[...], 1.0, 0.0).astype(jnp.bfloat16)
    out_ref[...] = dot(chosen, total.astype(jnp.bfloat16)).astype(jnp.bfloat16)


def head_grads(blk, parts, w_out, slot_row):
    return pl.pallas_call(
        head_grads_kernel,
        out_shape=jax.ShapeDtypeStruct((CLUSTERS * MOST, w_out.shape[0]), jnp.bfloat16),
        in_specs=[SMEM] + [VMEM] * 6,
        out_specs=VMEM,
        compiler_params=pltpu.CompilerParams(vmem_limit_bytes=GRANT),
        cost_estimate=cost(1),
        name="head_grads",
    )(blk, *parts, w_out, slot_row)


GROUP = 16


def spans(blk, width):
    return [pl.ds(pl.multiple_of(blk[j] * width, width), width) for j in range(4)]


def load_all(first, sources, targets, sems):
    @pl.when(first)
    def _():
        for source, target, i in zip(sources, targets, range(3)):
            pltpu.make_async_copy(source, target, sems.at[i]).start()


def wait_for(first, source, target, sem):
    @pl.when(first)
    def _():
        pltpu.make_async_copy(source, target, sem).wait()


def forward_kernel(blk, x0, x1, x2, x3, wq, wk, wv, *refs):
    mixed, saved, probs_ref, *loaded, sems = refs[-7:]
    sources, rows, width = x0.shape
    heads_width = wq.shape[1]
    heads = heads_width // HEAD_DIM
    scale = HEAD_DIM ** (-0.5)
    span = spans(blk, width)
    first = pl.program_id(0) == 0
    load_all(first, (wq, wk, wv), loaded, sems)
    members = sources * GROUP
    shape = (sources, GROUP, members)
    here = (iota(shape, 1) // MOST).reshape(members, members)
    source_here = iota(shape, 0).reshape(members, members)
    place_here = iota(shape, 1).reshape(members, members)
    lane = iota((members, members), 1)
    there = lane % GROUP // MOST
    same = here == there
    earlier = same & (lane // GROUP < source_here)
    later = same & (lane // GROUP > source_here)
    diagonal = source_here * GROUP + place_here == lane
    rank_col = (place_here % MOST).astype(jnp.float32)[:, :1]
    rank_row = (lane % MOST).astype(jnp.float32)[:1, :]
    groups = [slice(n * GROUP, (n + 1) * GROUP) for n in range(rows // GROUP)]
    kept, usable = ([], [])
    for group in groups:
        mark = x0[:, group, :HEAD_DIM].reshape(members, HEAD_DIM)[:, :1].astype(jnp.float32)
        held_col = jnp.where(mark <= LIMIT, 1.0, 0.0)
        held_row = jnp.sum(jnp.where(diagonal, held_col, 0.0), axis=0, keepdims=True)
        place_col = rank_col + jnp.sum(jnp.where(earlier, held_row, 0.0), axis=1, keepdims=True)
        place_row = rank_row + jnp.sum(jnp.where(later, held_col, 0.0), axis=0, keepdims=True)
        kept.append(jnp.where(place_col < CAP, held_col, 0.0))
        usable.append(same & (jnp.where(place_row < CAP, held_row, 0.0) > 0))

    xs = [r[...].reshape(sources * rows, width) for r in (x0, x1, x2, x3)]
    for i, (w, source) in enumerate(zip(loaded, (wq, wk, wv))):
        wait_for(first, source, w, sems.at[i])
        total = dot(xs[0], w[span[0], :])
        for j in range(1, 4):
            total = total + dot(xs[j], w[span[j], :])
        saved[:, :, i * heads_width : (i + 1) * heads_width] = total.astype(jnp.bfloat16).reshape(
            sources, rows, heads_width
        )

    def part(i, n, h):
        start = i * heads_width + h * HEAD_DIM
        return saved[:, groups[n], start : start + HEAD_DIM].reshape(members, HEAD_DIM)

    every = [(n, h) for n in range(len(groups)) for h in range(heads)]
    scores = [
        jnp.where(usable[n], dot(part(0, n, h), part(1, n, h), NT) * scale, -1e30)
        for n, h in every
    ]
    raised = [jnp.exp(s - jnp.max(s, axis=1, keepdims=True)) for s in scores]
    probs = [
        r * (kept[n] / jnp.sum(r, axis=1, keepdims=True)) for (n, h), r in zip(every, raised)
    ]
    for (n, h), p in zip(every, probs):
        probs_ref[0, n, h] = p
        out = dot(p.astype(jnp.bfloat16), part(2, n, h)).astype(jnp.bfloat16)
        mixed[:, groups[n], h * HEAD_DIM : (h + 1) * HEAD_DIM] = out.reshape(
            sources, GROUP, HEAD_DIM
        )


def backward_kernel(blk, saved, probs_ref, g_ref, wq, wk, wv, *refs):
    keep, give, (dq, dk, dv, *loaded, sems) = (refs[:2], refs[2:6], refs[6:])
    sources, rows, _ = saved.shape
    width = keep[0].shape[2]
    heads_width = wq.shape[1]
    heads = heads_width // HEAD_DIM
    scale = HEAD_DIM ** (-0.5)
    span = spans(blk, width)
    first = pl.program_id(0) == 0
    load_all(first, (wq, wk, wv), loaded, sems)
    members = sources * GROUP
    groups = [slice(n * GROUP, (n + 1) * GROUP) for n in range(rows // GROUP)]
    every = [(n, h) for n in range(len(groups)) for h in range(heads)]

    def part(i, n, h):
        start = i * heads_width + h * HEAD_DIM
        return saved[:, groups[n], start : start + HEAD_DIM].reshape(members, HEAD_DIM)

    def grad(n, h):
        return g_ref[:, groups[n], h * HEAD_DIM : (h + 1) * HEAD_DIM].reshape(members, HEAD_DIM)

    def put(ref, n, h, value):
        cols = slice(h * HEAD_DIM, (h + 1) * HEAD_DIM)
        ref[:, groups[n], cols] = value.astype(jnp.bfloat16).reshape(sources, GROUP, HEAD_DIM)

    grad_probs = [dot(grad(n, h), part(2, n, h), NT) for n, h in every]
    for n, h in every:
        put(dv, n, h, dot(probs_ref[0, n, h].astype(jnp.bfloat16), grad(n, h), TN))
    inner = [
        jnp.sum(gp * probs_ref[0, n, h], axis=1, keepdims=True)
        for (n, h), gp in zip(every, grad_probs)
    ]
    grad_scores = [
        (probs_ref[0, n, h] * (gp - i) * scale).astype(jnp.bfloat16)
        for (n, h), gp, i in zip(every, grad_probs, inner)
    ]
    for (n, h), gs in zip(every, grad_scores):
        put(dq, n, h, dot(gs, part(1, n, h)))
    for (n, h), gs in zip(every, grad_scores):
        put(dk, n, h, dot(gs, part(0, n, h), TN))
    for i, (w, source) in enumerate(zip(loaded, (wq, wk, wv))):
        wait_for(first, source, w, sems.at[i])
    grads = [d[...].reshape(sources * rows, heads_width) for d in (dq, dk, dv)]
    for j in (1, 3, 0, 2):
        total = None
        for d, w in zip(grads, loaded):
            term = dot(d, w[span[j], :], NT)
            total = term if total is None else total + term
        total = total.astype(jnp.bfloat16).reshape(sources, rows, width)
        if j % 2 == 0:
            keep[j // 2][...] = total
        else:
            give[j - 1][...] = total[: sources // 2]
            give[j][...] = total[sources // 2 :]


def step_of(sources, rows):
    step = GROUP
    while step * 2 * sources <= 256 and rows % (step * 2) == 0:
        step *= 2
    return step


def forward(blk, parts, wq, wk, wv, chunk, chunks, mixed):
    sources, rows, width = parts[2].shape
    heads_width = wq.shape[1]
    heads = heads_width // HEAD_DIM
    step = step_of(sources, rows)
    steps, groups, members = (rows // step, step // GROUP, sources * GROUP)
    block = pl.BlockSpec((sources, step, width), lambda p: (0, p, 0))
    whole = pl.BlockSpec((sources, step, width), lambda p: (0, p + chunk * steps, 0))
    weight = pl.BlockSpec(memory_space=pl.ANY)
    loaded = [pltpu.VMEM(wq.shape, wq.dtype)] * 3 + [pltpu.SemaphoreType.DMA((3,))]
    in_specs = [SMEM] + [whole] * 2 + [block] * 2 + [weight] * 3
    operands = [blk, *parts, wq, wk, wv]
    if mixed is not None:
        in_specs.append(pl.BlockSpec(memory_space=pl.ANY))
        operands.append(mixed)
    return pl.pallas_call(
        forward_kernel,
        grid=(steps,),
        out_shape=(
            jax.ShapeDtypeStruct((sources, rows * chunks, heads_width), jnp.bfloat16),
            jax.ShapeDtypeStruct((sources, rows, 3 * heads_width), jnp.bfloat16),
            jax.ShapeDtypeStruct((steps, groups, heads, members, members), jnp.float32),
        ),
        in_specs=in_specs,
        out_specs=(
            pl.BlockSpec((sources, step, heads_width), lambda p: (0, p + chunk * steps, 0)),
            pl.BlockSpec((sources, step, 3 * heads_width), lambda p: (0, p, 0)),
            pl.BlockSpec((1, groups, heads, members, members), lambda p: (p, 0, 0, 0, 0)),
        ),
        scratch_shapes=loaded,
        input_output_aliases={} if mixed is None else {len(operands) - 1: 0},
        compiler_params=pltpu.CompilerParams(vmem_limit_bytes=GRANT),
        cost_estimate=cost(6),
        name="forward",
    )(*operands)


def backward(blk, saved, probs, grads, wq, wk, wv, chunk):
    sources, rows, _ = saved.shape
    heads_width = wq.shape[1]
    width = wq.shape[0] // 4
    heads = heads_width // HEAD_DIM
    step = step_of(sources, rows)
    steps, groups, members = (rows // step, step // GROUP, sources * GROUP)
    block = pl.BlockSpec((sources, step, width), lambda p: (0, p, 0))
    half = pl.BlockSpec((sources // 2, step, width), lambda p: (0, p, 0))
    weight = pl.BlockSpec(memory_space=pl.ANY)
    loaded = [pltpu.VMEM(wq.shape, wq.dtype)] * 3 + [pltpu.SemaphoreType.DMA((3,))]
    shape = jax.ShapeDtypeStruct((sources, rows, width), jnp.bfloat16)
    half_shape = jax.ShapeDtypeStruct((sources // 2, rows, width), jnp.bfloat16)
    outs = pl.pallas_call(
        backward_kernel,
        grid=(steps,),
        out_shape=(shape,) * 2 + (half_shape,) * 4,
        in_specs=[
            SMEM,
            pl.BlockSpec((sources, step, 3 * heads_width), lambda p: (0, p, 0)),
            pl.BlockSpec((1, groups, heads, members, members), lambda p: (p, 0, 0, 0, 0)),
            pl.BlockSpec((sources, step, heads_width), lambda p: (0, p + chunk * steps, 0)),
            weight,
            weight,
            weight,
        ],
        out_specs=(block,) * 2 + (half,) * 4,
        scratch_shapes=[pltpu.VMEM((sources, step, heads_width), jnp.bfloat16)] * 3 + loaded,
        compiler_params=pltpu.CompilerParams(vmem_limit_bytes=GRANT),
        cost_estimate=cost(6),
        name="backward",
    )(blk, saved, probs, grads, wq, wk, wv)
    return (outs[:2], outs[2:])


def slab(w, blk, j):
    width = w.shape[0] // 4
    return lax.dynamic_slice_in_dim(w, blk[j] * width, width, 0)


def by_cluster(x):
    sources, rows = x.shape[:2]
    x = x.reshape(sources, rows // MOST, MOST, -1).transpose(1, 0, 2, 3)
    return x.reshape(rows // MOST, sources * MOST, -1)


def by_source(x, sources):
    clusters = x.shape[0]
    x = x.reshape(clusters, sources, MOST, -1).transpose(1, 0, 2, 3)
    return x.reshape(sources, clusters * MOST, -1)


def split_heads(x):
    return x.reshape(x.shape[0], -1, HEAD_DIM)


ein = functools.partial(jnp.einsum, preferred_element_type=jnp.float32)


def forward_many(blk, parts, wq, wk, wv):
    sources, rows, _ = parts[0].shape

    def project(w):
        total = 0.0
        for j in range(4):
            total = total + ein("srd,dh->srh", parts[j], slab(w, blk, j))
        return by_cluster(total.astype(jnp.bfloat16))

    held = (parts[0][:, :, 0].astype(jnp.float32) <= LIMIT).reshape(sources, -1, MOST)
    counts = jnp.sum(held.astype(jnp.int32), axis=2, keepdims=True)
    rank = jnp.cumsum(counts, axis=0) - counts + jnp.arange(MOST)
    kept = by_cluster((held & (rank < CAP)).astype(jnp.float32).reshape(sources, rows, 1))
    scale = HEAD_DIM ** (-0.5)

    def one(args):
        q, k, v, live = args
        q, k, v = (split_heads(a) for a in (q, k, v))
        scores = jnp.where(live[None, None, :, 0] > 0, ein("qhd,khd->hqk", q, k) * scale, -1e30)
        raised = jnp.exp(scores - jnp.max(scores, axis=-1, keepdims=True))
        probs = raised * (live / jnp.sum(raised, axis=-1, keepdims=True))
        mixed = ein("hqk,khd->qhd", probs.astype(jnp.bfloat16), v).astype(jnp.bfloat16)
        return (mixed.reshape(mixed.shape[0], -1), probs)

    saved = tuple(project(w) for w in (wq, wk, wv))
    mixed, probs = lax.map(one, saved + (kept,))
    return (by_source(mixed, sources), saved, probs)


def backward_many(blk, saved, probs, grads, wq, wk, wv):
    sources = grads.shape[0]
    scale = HEAD_DIM ** (-0.5)

    def one(args):
        q, k, v, probs, g = args
        q, k, v, g = (split_heads(a) for a in (q, k, v, g))
        dv = ein("hqk,qhd->khd", probs.astype(jnp.bfloat16), g)
        grad_probs = ein("qhd,khd->hqk", g, v)
        inner = jnp.sum(grad_probs * probs, axis=-1, keepdims=True)
        grad_scores = (probs * (grad_probs - inner) * scale).astype(jnp.bfloat16)
        dq = ein("hqk,khd->qhd", grad_scores, k)
        dk = ein("hqk,qhd->khd", grad_scores, q)
        return tuple(a.astype(jnp.bfloat16).reshape(a.shape[0], -1) for a in (dq, dk, dv))

    dq, dk, dv = lax.map(one, saved + (probs, by_cluster(grads)))
    outs = []
    for j in range(4):
        total = 0.0
        for d, w in ((dq, wq), (dk, wk), (dv, wv)):
            total = total + ein("crh,wh->crw", d, slab(w, blk, j))
        outs.append(by_source(total.astype(jnp.bfloat16), sources))
    half = sources // 2
    return ((outs[0], outs[2]), (outs[1][:half], outs[1][half:], outs[3][:half], outs[3][half:]))


def pick(slot_col, slots):
    held = iota((1, slots.shape[0]), 1) == slot_col[...]
    return dot(jnp.where(held, 1.0, 0.0).astype(jnp.bfloat16), slots[...])


def out_kernel(blk, slot_col, w_out, mixed, *outs):
    keep, give = (outs[:2], outs[2:])
    heads = pick(slot_col, mixed).astype(jnp.bfloat16)
    tokens, width = keep[0].shape
    span = spans(blk, width)
    for j in (1, 3, 0, 2):
        total = dot(heads, w_out[:, span[j]]).astype(jnp.bfloat16)
        if j % 2 == 0:
            keep[j // 2][...] = total
        else:
            give[j - 1][...] = total[: tokens // 2]
            give[j][...] = total[tokens // 2 :]


def project_out(blk, slot_col, w_out, mixed):
    tokens, width = (slot_col.shape[0], w_out.shape[1] // 4)
    shape = jax.ShapeDtypeStruct((tokens, width), jnp.bfloat16)
    half = jax.ShapeDtypeStruct((tokens // 2, width), jnp.bfloat16)
    outs = pl.pallas_call(
        out_kernel,
        out_shape=(shape,) * 2 + (half,) * 4,
        in_specs=[SMEM] + [VMEM] * 3,
        out_specs=(VMEM,) * 6,
        compiler_params=pltpu.CompilerParams(vmem_limit_bytes=GRANT),
        cost_estimate=cost(6),
        name="project_out",
    )(blk, slot_col, w_out, mixed)
    return (outs[:2], outs[2:])


def final_kernel(slot_col, slots, out):
    out[...] = pick(slot_col, slots)


def to_tokens(slot_col, slots):
    return pl.pallas_call(
        final_kernel,
        out_shape=jax.ShapeDtypeStruct((slot_col.shape[0], slots.shape[1]), jnp.float32),
        compiler_params=pltpu.CompilerParams(vmem_limit_bytes=GRANT),
        cost_estimate=cost(1),
        name="to_tokens",
    )(slot_col, slots)


def wide(x):
    return x.astype(jnp.float32)


def add_kernel(*refs):
    whole, halves, more, out = (refs[0], refs[1:3], refs[3:-1], refs[-1])
    size = whole.shape[0] // 2
    for i, half in enumerate(halves):
        rows = slice(i * size, (i + 1) * size)
        total = wide(whole[rows]) + wide(half[...])
        if more:
            total = total + wide(more[0][rows])
        out[rows] = total.astype(jnp.bfloat16)


def add(whole, first, second, *more, into=None, chunk=0, chunks=1):
    shape = whole.shape
    block = pl.BlockSpec(shape, lambda p: (0,) * len(shape))
    half = pl.BlockSpec(first.shape, lambda p: (0,) * len(shape))
    place = (0, chunk, 0)[: len(shape)]
    full = (shape[0], shape[1] * chunks) + shape[2:] if chunks > 1 else shape
    operands = [whole, first, second, *more]
    in_specs = [block, half, half] + [block] * len(more)
    kernel, aliases = (add_kernel, {})
    if into is not None:
        aliases = {len(operands): 0}
        operands.append(into)
        in_specs.append(pl.BlockSpec(memory_space=pl.ANY))

        def kernel(*refs):
            add_kernel(*refs[:-2], refs[-1])

    return pl.pallas_call(
        kernel,
        grid=(1,),
        out_shape=jax.ShapeDtypeStruct(full, jnp.bfloat16),
        in_specs=in_specs,
        out_specs=pl.BlockSpec(shape, lambda p: place if chunks > 1 else (0,) * len(shape)),
        input_output_aliases=aliases,
        compiler_params=pltpu.CompilerParams(vmem_limit_bytes=GRANT),
        cost_estimate=cost(0.001),
        name="add",
    )(*operands)


def reduce_pairs(keep, give):
    got = [swap(x, 1) for x in give]
    return (keep[0], got[:2], add(keep[1], *got[2:]))


def body(normed, cluster, w_query, w_key, w_value, w_out, grad_out):
    seq_count = lax.axis_size("seq")
    per = CLUSTERS // seq_count * MOST
    chunks = CHUNKS if per // CHUNKS % GROUP == 0 else 1
    rows = per // chunks
    blk = lax.axis_index("tp") ^ jnp.arange(4, dtype=jnp.int32)
    weights = (w_query, w_key, w_value)
    small = seq_count * GROUP <= 256

    g_across = swap(grad_out, 2)
    g_parts = (grad_out, swap(grad_out, 1), g_across, swap(g_across, 1))
    slot_col, slot_row, x_slots = place(cluster, normed)
    x = exchange(x_slots.reshape(seq_count, per, -1))
    g_slots = head_grads(blk, g_parts, w_out, slot_row).reshape(seq_count, per, -1)
    x = after(x, g_slots)
    g = exchange(after(g_slots, x))

    x_core, x_across = (swap(x, 1), [])
    for c in range(chunks):
        piece = x[:, c * rows : (c + 1) * rows]
        x_across.append(swap(piece, 2))
    mixed, saved = (None, [])
    for c in range(chunks):
        if c > 0:
            x_across[c] = after(x_across[c], mixed)
        parts = (x, x_core, x_across[c], swap(x_across[c], 1))
        if c > 0:
            parts = (after(x, g),) + parts[1:]
        if small:
            mixed, *kept = forward(blk, parts, *weights, c, chunks, mixed)
        else:
            mixed, *kept = forward_many(blk, parts, *weights)
        saved.append(kept)
    mixed_back = exchange(after(mixed, g))

    g = after(g, mixed)
    for c in range(chunks):
        if small:
            keep, give = backward(blk, *saved[c], g, *weights, c)
        else:
            keep, give = backward_many(blk, *saved[c], g, *weights)
        keep, got, partial = reduce_pairs(keep, give)
        g = after(g, partial)
        if c > 0:
            partial = after(partial, saved[c - 1][3])
        saved[c] = (keep, *got, swap(partial, 2))
    summed = None
    for c in range(chunks):
        summed = add(*saved[c], into=summed, chunk=c, chunks=chunks)
    back = exchange(after(summed, mixed_back))
    keep, give = project_out(blk, slot_col, w_out, mixed_back.reshape(CLUSTERS * MOST, -1))
    keep, got, partial = reduce_pairs(keep, give)
    attended = add(keep, *got, swap(partial, 2))
    return (attended, to_tokens(slot_col, back.reshape(CLUSTERS * MOST, -1)))


def solution(mesh):
    in_specs = (
        P("seq", "tp"),
        P("seq", None),
        P(None, "tp"),
        P(None, "tp"),
        P(None, "tp"),
        P("tp", None),
        P("seq", "tp"),
    )
    out_specs = (P("seq", "tp"), P("seq", "tp"))
    return jax.shard_map(body, mesh=mesh, in_specs=in_specs, out_specs=out_specs, check_vma=False)
```

```python
import functools
import jax
import jax.numpy as jnp
from jax import lax
from jax.experimental import pallas as pl
from jax.experimental.pallas import tpu as pltpu
from jax.sharding import PartitionSpec as P

HEAD_DIM = 128
CLUSTERS = 128
CAP = 256
MOST = 8
LIMIT = 24.0
EMPTY = 32.0
NN = (((1,), (0,)), ((), ()))
NT = (((1,), (1,)), ((), ()))
TN = (((0,), (0,)), ((), ()))
MB = 1024 * 1024
CHUNKS = 2
GRANT = 24 * MB


def cost(giga):
    return pl.CostEstimate(flops=int(giga * 1e9), bytes_accessed=MB, transcendentals=0)


VMEM = pl.BlockSpec(memory_space=pltpu.VMEM)
SMEM = pl.BlockSpec(memory_space=pltpu.SMEM)


def dot(a, b, dims=NN):
    return lax.dot_general(a, b, dims, preferred_element_type=jnp.float32)


def iota(shape, dim):
    return lax.broadcasted_iota(jnp.int32, shape, dim)


def swap(x, bit):
    count = lax.axis_size("tp")
    return lax.ppermute(x, "tp", [(i, i ^ bit) for i in range(count)])


def exchange(x):
    return lax.all_to_all(x, "seq", split_axis=0, concat_axis=0, tiled=True)


def after(x, *others):
    return lax.optimization_barrier((x,) + others)[0]


def place_kernel(ids_col, x_ref, slot_col, slot_row, out):
    tokens = x_ref.shape[0]
    here, there = (iota((tokens, tokens), 0), iota((tokens, tokens), 1))
    col = ids_col[...]
    row = jnp.sum(jnp.where(here == there, col, 0), axis=0, keepdims=True)
    same = col == row
    earlier = jnp.where(same & (there < here), 1.0, 0.0)
    later = jnp.where(same & (here < there), 1.0, 0.0)
    slot_col[...] = col * MOST + jnp.sum(earlier, axis=1, keepdims=True).astype(jnp.int32)
    slot_row[...] = row * MOST + jnp.sum(later, axis=0, keepdims=True).astype(jnp.int32)
    slots, width = out.shape
    chosen = jnp.where(iota((slots, tokens), 0) == slot_row[...], 1.0, 0.0)
    taken = jnp.sum(chosen, axis=1, keepdims=True)
    value = dot(chosen.astype(jnp.bfloat16), x_ref[...])
    first = iota((slots, width), 1) == 0
    out[...] = (value + jnp.where(first & (taken == 0.0), EMPTY, 0.0)).astype(jnp.bfloat16)


def place(cluster, x):
    tokens = x.shape[0]
    return pl.pallas_call(
        place_kernel,
        out_shape=(
            jax.ShapeDtypeStruct((tokens, 1), jnp.int32),
            jax.ShapeDtypeStruct((1, tokens), jnp.int32),
            jax.ShapeDtypeStruct((CLUSTERS * MOST, x.shape[1]), jnp.bfloat16),
        ),
        compiler_params=pltpu.CompilerParams(vmem_limit_bytes=GRANT),
        cost_estimate=cost(1),
        name="place",
    )(cluster, x)


def head_grads_kernel(blk, a0, a1, a2, a3, w_out, slot_row, out_ref):
    width = a0.shape[1]
    total = None
    for j, part in enumerate((a0, a1, a2, a3)):
        cols = pl.ds(pl.multiple_of(blk[j] * width, width), width)
        term = dot(part[...], w_out[:, cols], NT)
        total = term if total is None else total + term
    slots, tokens = (out_ref.shape[0], a0.shape[0])
    chosen = jnp.where(iota((slots, tokens), 0) == slot_row[...], 1.0, 0.0).astype(jnp.bfloat16)
    out_ref[...] = dot(chosen, total.astype(jnp.bfloat16)).astype(jnp.bfloat16)


def head_grads(blk, parts, w_out, slot_row):
    return pl.pallas_call(
        head_grads_kernel,
        out_shape=jax.ShapeDtypeStruct((CLUSTERS * MOST, w_out.shape[0]), jnp.bfloat16),
        in_specs=[SMEM] + [VMEM] * 6,
        out_specs=VMEM,
        compiler_params=pltpu.CompilerParams(vmem_limit_bytes=GRANT),
        cost_estimate=cost(1),
        name="head_grads",
    )(blk, *parts, w_out, slot_row)


GROUP = 16


def spans(blk, width):
    return [pl.ds(pl.multiple_of(blk[j] * width, width), width) for j in range(4)]


def load_all(first, sources, targets, sems):
    @pl.when(first)
    def _():
        for source, target, i in zip(sources, targets, range(3)):
            pltpu.make_async_copy(source, target, sems.at[i]).start()


def wait_for(first, source, target, sem):
    @pl.when(first)
    def _():
        pltpu.make_async_copy(source, target, sem).wait()


def forward_kernel(blk, x0, x1, x2, x3, wq, wk, wv, *refs):
    mixed, saved, probs_ref = refs[-3:]
    sources, rows, width = x0.shape
    heads_width = wq.shape[1]
    heads = heads_width // HEAD_DIM
    scale = HEAD_DIM ** (-0.5)
    span = spans(blk, width)
    members = sources * GROUP
    shape = (sources, GROUP, members)
    here = (iota(shape, 1) // MOST).reshape(members, members)
    source_here = iota(shape, 0).reshape(members, members)
    place_here = iota(shape, 1).reshape(members, members)
    lane = iota((members, members), 1)
    there = lane % GROUP // MOST
    same = here == there
    earlier = same & (lane // GROUP < source_here)
    later = same & (lane // GROUP > source_here)
    diagonal = source_here * GROUP + place_here == lane
    rank_col = (place_here % MOST).astype(jnp.float32)[:, :1]
    rank_row = (lane % MOST).astype(jnp.float32)[:1, :]
    groups = [slice(n * GROUP, (n + 1) * GROUP) for n in range(rows // GROUP)]
    kept, usable = ([], [])
    for group in groups:
        mark = x0[:, group, :HEAD_DIM].reshape(members, HEAD_DIM)[:, :1].astype(jnp.float32)
        held_col = jnp.where(mark <= LIMIT, 1.0, 0.0)
        held_row = jnp.sum(jnp.where(diagonal, held_col, 0.0), axis=0, keepdims=True)
        place_col = rank_col + jnp.sum(jnp.where(earlier, held_row, 0.0), axis=1, keepdims=True)
        place_row = rank_row + jnp.sum(jnp.where(later, held_col, 0.0), axis=0, keepdims=True)
        kept.append(jnp.where(place_col < CAP, held_col, 0.0))
        usable.append(same & (jnp.where(place_row < CAP, held_row, 0.0) > 0))

    xs = [r[...].reshape(sources * rows, width) for r in (x0, x1, x2, x3)]
    for i, w in enumerate((wq, wk, wv)):
        total = dot(xs[0], w[span[0], :])
        for j in range(1, 4):
            total = total + dot(xs[j], w[span[j], :])
        saved[:, :, i * heads_width : (i + 1) * heads_width] = total.astype(jnp.bfloat16).reshape(
            sources, rows, heads_width
        )

    def part(i, n, h):
        start = i * heads_width + h * HEAD_DIM
        return saved[:, groups[n], start : start + HEAD_DIM].reshape(members, HEAD_DIM)

    every = [(n, h) for n in range(len(groups)) for h in range(heads)]
    scores = [
        jnp.where(usable[n], dot(part(0, n, h), part(1, n, h), NT) * scale, -1e30)
        for n, h in every
    ]
    raised = [jnp.exp(s - jnp.max(s, axis=1, keepdims=True)) for s in scores]
    probs = [
        r * (kept[n] / jnp.sum(r, axis=1, keepdims=True)) for (n, h), r in zip(every, raised)
    ]
    for (n, h), p in zip(every, probs):
        probs_ref[0, n, h] = p
        out = dot(p.astype(jnp.bfloat16), part(2, n, h)).astype(jnp.bfloat16)
        mixed[:, groups[n], h * HEAD_DIM : (h + 1) * HEAD_DIM] = out.reshape(
            sources, GROUP, HEAD_DIM
        )


def backward_kernel(blk, saved, probs_ref, g_ref, wq, wk, wv, *refs):
    keep, give, (dq, dk, dv) = (refs[:2], refs[2:6], refs[6:])
    sources, rows, _ = saved.shape
    width = keep[0].shape[2]
    heads_width = wq.shape[1]
    heads = heads_width // HEAD_DIM
    scale = HEAD_DIM ** (-0.5)
    span = spans(blk, width)
    members = sources * GROUP
    groups = [slice(n * GROUP, (n + 1) * GROUP) for n in range(rows // GROUP)]
    every = [(n, h) for n in range(len(groups)) for h in range(heads)]

    def part(i, n, h):
        start = i * heads_width + h * HEAD_DIM
        return saved[:, groups[n], start : start + HEAD_DIM].reshape(members, HEAD_DIM)

    def grad(n, h):
        return g_ref[:, groups[n], h * HEAD_DIM : (h + 1) * HEAD_DIM].reshape(members, HEAD_DIM)

    def put(ref, n, h, value):
        cols = slice(h * HEAD_DIM, (h + 1) * HEAD_DIM)
        ref[:, groups[n], cols] = value.astype(jnp.bfloat16).reshape(sources, GROUP, HEAD_DIM)

    grad_probs = [dot(grad(n, h), part(2, n, h), NT) for n, h in every]
    for n, h in every:
        put(dv, n, h, dot(probs_ref[0, n, h].astype(jnp.bfloat16), grad(n, h), TN))
    inner = [
        jnp.sum(gp * probs_ref[0, n, h], axis=1, keepdims=True)
        for (n, h), gp in zip(every, grad_probs)
    ]
    grad_scores = [
        (probs_ref[0, n, h] * (gp - i) * scale).astype(jnp.bfloat16)
        for (n, h), gp, i in zip(every, grad_probs, inner)
    ]
    for (n, h), gs in zip(every, grad_scores):
        put(dq, n, h, dot(gs, part(1, n, h)))
    for (n, h), gs in zip(every, grad_scores):
        put(dk, n, h, dot(gs, part(0, n, h), TN))
    grads = [d[...].reshape(sources * rows, heads_width) for d in (dq, dk, dv)]
    for j in (1, 3, 0, 2):
        total = None
        for d, w in zip(grads, (wq, wk, wv)):
            term = dot(d, w[span[j], :], NT)
            total = term if total is None else total + term
        total = total.astype(jnp.bfloat16).reshape(sources, rows, width)
        if j % 2 == 0:
            keep[j // 2][...] = total
        else:
            give[j - 1][...] = total[: sources // 2]
            give[j][...] = total[sources // 2 :]


def step_of(sources, rows):
    step = GROUP
    while step * 2 * sources <= 256 and rows % (step * 2) == 0:
        step *= 2
    return step


def forward(blk, parts, wq, wk, wv, chunk, chunks, mixed):
    sources, rows, width = parts[2].shape
    heads_width = wq.shape[1]
    heads = heads_width // HEAD_DIM
    step = step_of(sources, rows)
    steps, groups, members = (rows // step, step // GROUP, sources * GROUP)
    block = pl.BlockSpec((sources, step, width), lambda p: (0, p, 0))
    whole = pl.BlockSpec((sources, step, width), lambda p: (0, p + chunk * steps, 0))
    weight = VMEM
    in_specs = [SMEM] + [whole] * 2 + [block] * 2 + [weight] * 3
    operands = [blk, *parts, wq, wk, wv]
    if mixed is not None:
        in_specs.append(pl.BlockSpec(memory_space=pl.ANY))
        operands.append(mixed)
    return pl.pallas_call(
        forward_kernel,
        grid=(steps,),
        out_shape=(
            jax.ShapeDtypeStruct((sources, rows * chunks, heads_width), jnp.bfloat16),
            jax.ShapeDtypeStruct((sources, rows, 3 * heads_width), jnp.bfloat16),
            jax.ShapeDtypeStruct((steps, groups, heads, members, members), jnp.float32),
        ),
        in_specs=in_specs,
        out_specs=(
            pl.BlockSpec((sources, step, heads_width), lambda p: (0, p + chunk * steps, 0)),
            pl.BlockSpec((sources, step, 3 * heads_width), lambda p: (0, p, 0)),
            pl.BlockSpec((1, groups, heads, members, members), lambda p: (p, 0, 0, 0, 0)),
        ),
        input_output_aliases={} if mixed is None else {len(operands) - 1: 0},
        compiler_params=pltpu.CompilerParams(vmem_limit_bytes=GRANT),
        cost_estimate=cost(1),
        name="forward",
    )(*operands)


def backward(blk, saved, probs, grads, wq, wk, wv, chunk):
    sources, rows, _ = saved.shape
    heads_width = wq.shape[1]
    width = wq.shape[0] // 4
    heads = heads_width // HEAD_DIM
    step = step_of(sources, rows)
    steps, groups, members = (rows // step, step // GROUP, sources * GROUP)
    block = pl.BlockSpec((sources, step, width), lambda p: (0, p, 0))
    half = pl.BlockSpec((sources // 2, step, width), lambda p: (0, p, 0))
    weight = VMEM
    shape = jax.ShapeDtypeStruct((sources, rows, width), jnp.bfloat16)
    half_shape = jax.ShapeDtypeStruct((sources // 2, rows, width), jnp.bfloat16)
    outs = pl.pallas_call(
        backward_kernel,
        grid=(steps,),
        out_shape=(shape,) * 2 + (half_shape,) * 4,
        in_specs=[
            SMEM,
            pl.BlockSpec((sources, step, 3 * heads_width), lambda p: (0, p, 0)),
            pl.BlockSpec((1, groups, heads, members, members), lambda p: (p, 0, 0, 0, 0)),
            pl.BlockSpec((sources, step, heads_width), lambda p: (0, p + chunk * steps, 0)),
            weight,
            weight,
            weight,
        ],
        out_specs=(block,) * 2 + (half,) * 4,
        scratch_shapes=[pltpu.VMEM((sources, step, heads_width), jnp.bfloat16)] * 3,
        compiler_params=pltpu.CompilerParams(vmem_limit_bytes=GRANT),
        cost_estimate=cost(1),
        name="backward",
    )(blk, saved, probs, grads, wq, wk, wv)
    return (outs[:2], outs[2:])


def slab(w, blk, j):
    width = w.shape[0] // 4
    return lax.dynamic_slice_in_dim(w, blk[j] * width, width, 0)


def by_cluster(x):
    sources, rows = x.shape[:2]
    x = x.reshape(sources, rows // MOST, MOST, -1).transpose(1, 0, 2, 3)
    return x.reshape(rows // MOST, sources * MOST, -1)


def by_source(x, sources):
    clusters = x.shape[0]
    x = x.reshape(clusters, sources, MOST, -1).transpose(1, 0, 2, 3)
    return x.reshape(sources, clusters * MOST, -1)


def split_heads(x):
    return x.reshape(x.shape[0], -1, HEAD_DIM)


ein = functools.partial(jnp.einsum, preferred_element_type=jnp.float32)


def forward_many(blk, parts, wq, wk, wv):
    sources, rows, _ = parts[0].shape

    def project(w):
        total = 0.0
        for j in range(4):
            total = total + ein("srd,dh->srh", parts[j], slab(w, blk, j))
        return by_cluster(total.astype(jnp.bfloat16))

    held = (parts[0][:, :, 0].astype(jnp.float32) <= LIMIT).reshape(sources, -1, MOST)
    counts = jnp.sum(held.astype(jnp.int32), axis=2, keepdims=True)
    rank = jnp.cumsum(counts, axis=0) - counts + jnp.arange(MOST)
    kept = by_cluster((held & (rank < CAP)).astype(jnp.float32).reshape(sources, rows, 1))
    scale = HEAD_DIM ** (-0.5)

    def one(args):
        q, k, v, live = args
        q, k, v = (split_heads(a) for a in (q, k, v))
        scores = jnp.where(live[None, None, :, 0] > 0, ein("qhd,khd->hqk", q, k) * scale, -1e30)
        raised = jnp.exp(scores - jnp.max(scores, axis=-1, keepdims=True))
        probs = raised * (live / jnp.sum(raised, axis=-1, keepdims=True))
        mixed = ein("hqk,khd->qhd", probs.astype(jnp.bfloat16), v).astype(jnp.bfloat16)
        return (mixed.reshape(mixed.shape[0], -1), probs)

    saved = tuple(project(w) for w in (wq, wk, wv))
    mixed, probs = lax.map(one, saved + (kept,))
    return (by_source(mixed, sources), saved, probs)


def backward_many(blk, saved, probs, grads, wq, wk, wv):
    sources = grads.shape[0]
    scale = HEAD_DIM ** (-0.5)

    def one(args):
        q, k, v, probs, g = args
        q, k, v, g = (split_heads(a) for a in (q, k, v, g))
        dv = ein("hqk,qhd->khd", probs.astype(jnp.bfloat16), g)
        grad_probs = ein("qhd,khd->hqk", g, v)
        inner = jnp.sum(grad_probs * probs, axis=-1, keepdims=True)
        grad_scores = (probs * (grad_probs - inner) * scale).astype(jnp.bfloat16)
        dq = ein("hqk,khd->qhd", grad_scores, k)
        dk = ein("hqk,qhd->khd", grad_scores, q)
        return tuple(a.astype(jnp.bfloat16).reshape(a.shape[0], -1) for a in (dq, dk, dv))

    dq, dk, dv = lax.map(one, saved + (probs, by_cluster(grads)))
    outs = []
    for j in range(4):
        total = 0.0
        for d, w in ((dq, wq), (dk, wk), (dv, wv)):
            total = total + ein("crh,wh->crw", d, slab(w, blk, j))
        outs.append(by_source(total.astype(jnp.bfloat16), sources))
    half = sources // 2
    return ((outs[0], outs[2]), (outs[1][:half], outs[1][half:], outs[3][:half], outs[3][half:]))


def pick(slot_col, slots):
    held = iota((1, slots.shape[0]), 1) == slot_col[...]
    return dot(jnp.where(held, 1.0, 0.0).astype(jnp.bfloat16), slots[...])


def out_kernel(blk, slot_col, w_out, mixed, *outs):
    keep, give = (outs[:2], outs[2:])
    heads = pick(slot_col, mixed).astype(jnp.bfloat16)
    tokens, width = keep[0].shape
    span = spans(blk, width)
    for j in (1, 3, 0, 2):
        total = dot(heads, w_out[:, span[j]]).astype(jnp.bfloat16)
        if j % 2 == 0:
            keep[j // 2][...] = total
        else:
            give[j - 1][...] = total[: tokens // 2]
            give[j][...] = total[tokens // 2 :]


def project_out(blk, slot_col, w_out, mixed):
    tokens, width = (slot_col.shape[0], w_out.shape[1] // 4)
    shape = jax.ShapeDtypeStruct((tokens, width), jnp.bfloat16)
    half = jax.ShapeDtypeStruct((tokens // 2, width), jnp.bfloat16)
    outs = pl.pallas_call(
        out_kernel,
        out_shape=(shape,) * 2 + (half,) * 4,
        in_specs=[SMEM] + [VMEM] * 3,
        out_specs=(VMEM,) * 6,
        compiler_params=pltpu.CompilerParams(vmem_limit_bytes=GRANT),
        cost_estimate=cost(1),
        name="project_out",
    )(blk, slot_col, w_out, mixed)
    return (outs[:2], outs[2:])


def final_kernel(slot_col, slots, out):
    out[...] = pick(slot_col, slots)


def to_tokens(slot_col, slots):
    return pl.pallas_call(
        final_kernel,
        out_shape=jax.ShapeDtypeStruct((slot_col.shape[0], slots.shape[1]), jnp.float32),
        compiler_params=pltpu.CompilerParams(vmem_limit_bytes=GRANT),
        cost_estimate=cost(1),
        name="to_tokens",
    )(slot_col, slots)


def wide(x):
    return x.astype(jnp.float32)


def add_kernel(*refs):
    whole, halves, more, out = (refs[0], refs[1:3], refs[3:-1], refs[-1])
    size = whole.shape[0] // 2
    for i, half in enumerate(halves):
        rows = slice(i * size, (i + 1) * size)
        total = wide(whole[rows]) + wide(half[...])
        if more:
            total = total + wide(more[0][rows])
        out[rows] = total.astype(jnp.bfloat16)


def add(whole, first, second, *more, into=None, chunk=0, chunks=1):
    shape = whole.shape
    block = pl.BlockSpec(shape, lambda p: (0,) * len(shape))
    half = pl.BlockSpec(first.shape, lambda p: (0,) * len(shape))
    place = (0, chunk, 0)[: len(shape)]
    full = (shape[0], shape[1] * chunks) + shape[2:] if chunks > 1 else shape
    operands = [whole, first, second, *more]
    in_specs = [block, half, half] + [block] * len(more)
    kernel, aliases = (add_kernel, {})
    if into is not None:
        aliases = {len(operands): 0}
        operands.append(into)
        in_specs.append(pl.BlockSpec(memory_space=pl.ANY))

        def kernel(*refs):
            add_kernel(*refs[:-2], refs[-1])

    return pl.pallas_call(
        kernel,
        grid=(1,),
        out_shape=jax.ShapeDtypeStruct(full, jnp.bfloat16),
        in_specs=in_specs,
        out_specs=pl.BlockSpec(shape, lambda p: place if chunks > 1 else (0,) * len(shape)),
        input_output_aliases=aliases,
        compiler_params=pltpu.CompilerParams(vmem_limit_bytes=GRANT),
        cost_estimate=cost(0.001),
        name="add",
    )(*operands)


def reduce_pairs(keep, give):
    got = [swap(x, 1) for x in give]
    return (keep[0], got[:2], add(keep[1], *got[2:]))


def body(normed, cluster, w_query, w_key, w_value, w_out, grad_out):
    seq_count = lax.axis_size("seq")
    per = CLUSTERS // seq_count * MOST
    chunks = CHUNKS if per // CHUNKS % GROUP == 0 else 1
    rows = per // chunks
    blk = lax.axis_index("tp") ^ jnp.arange(4, dtype=jnp.int32)
    weights = (w_query, w_key, w_value)
    small = seq_count * GROUP <= 256

    g_across = swap(grad_out, 2)
    g_parts = (grad_out, swap(grad_out, 1), g_across, swap(g_across, 1))
    slot_col, slot_row, x_slots = place(cluster, normed)
    x = exchange(x_slots.reshape(seq_count, per, -1))
    g_slots = head_grads(blk, g_parts, w_out, slot_row).reshape(seq_count, per, -1)
    x = after(x, g_slots)
    g = exchange(after(g_slots, x))

    x_core, x_across = (swap(x, 1), [])
    for c in range(chunks):
        piece = x[:, c * rows : (c + 1) * rows]
        x_across.append(swap(piece, 2))
    mixed, saved = (None, [])
    for c in range(chunks):
        if c > 0:
            x_across[c] = after(x_across[c], mixed)
        parts = (x, x_core, x_across[c], swap(x_across[c], 1))
        if small:
            mixed, *kept = forward(blk, parts, *weights, c, chunks, mixed)
        else:
            mixed, *kept = forward_many(blk, parts, *weights)
        saved.append(kept)
    mixed_back = exchange(after(mixed, g))

    g = after(g, mixed)
    for c in range(chunks):
        if small:
            keep, give = backward(blk, *saved[c], g, *weights, c)
        else:
            keep, give = backward_many(blk, *saved[c], g, *weights)
        keep, got, partial = reduce_pairs(keep, give)
        g = after(g, partial)
        if c > 0:
            partial = after(partial, saved[c - 1][3])
        saved[c] = (keep, *got, swap(partial, 2))
    summed = None
    for c in range(chunks):
        summed = add(*saved[c], into=summed, chunk=c, chunks=chunks)
    back = exchange(after(summed, mixed_back))
    keep, give = project_out(blk, slot_col, w_out, mixed_back.reshape(CLUSTERS * MOST, -1))
    keep, got, partial = reduce_pairs(keep, give)
    attended = add(keep, *got, swap(partial, 2))
    return (attended, to_tokens(slot_col, back.reshape(CLUSTERS * MOST, -1)))


def solution(mesh):
    in_specs = (
        P("seq", "tp"),
        P("seq", None),
        P(None, "tp"),
        P(None, "tp"),
        P(None, "tp"),
        P("tp", None),
        P("seq", "tp"),
    )
    out_specs = (P("seq", "tp"), P("seq", "tp"))
    return jax.shard_map(body, mesh=mesh, in_specs=in_specs, out_specs=out_specs, check_vma=False)
```

```python
import functools
import jax
import jax.numpy as jnp
from jax import lax
from jax.experimental import pallas as pl
from jax.experimental.pallas import tpu as pltpu
from jax.sharding import PartitionSpec as P

HEAD_DIM = 128
CLUSTERS = 128
CAP = 256
MOST = 8
LIMIT = 24.0
EMPTY = 32.0
NN = (((1,), (0,)), ((), ()))
NT = (((1,), (1,)), ((), ()))
TN = (((0,), (0,)), ((), ()))
MB = 1024 * 1024
CHUNKS = 2
GRANT = 24 * MB


def cost(giga):
    return pl.CostEstimate(flops=int(giga * 1e9), bytes_accessed=MB, transcendentals=0)


VMEM = pl.BlockSpec(memory_space=pltpu.VMEM)
SMEM = pl.BlockSpec(memory_space=pltpu.SMEM)


def dot(a, b, dims=NN):
    return lax.dot_general(a, b, dims, preferred_element_type=jnp.float32)


def iota(shape, dim):
    return lax.broadcasted_iota(jnp.int32, shape, dim)


def swap(x, bit):
    count = lax.axis_size("tp")
    return lax.ppermute(x, "tp", [(i, i ^ bit) for i in range(count)])


def exchange(x):
    return lax.all_to_all(x, "seq", split_axis=0, concat_axis=0, tiled=True)


def after(x, *others):
    return lax.optimization_barrier((x,) + others)[0]


def slots_of(out, tokens, chunk, chunks):
    owners, rows, _ = out.shape
    shape = (owners, rows, tokens)
    slot = iota(shape, 0) * (rows * chunks) + iota(shape, 1) + chunk * rows
    return slot.reshape(owners * rows, tokens)


def place_kernel(ids_col, x_ref, slot_col, slot_row, *outs):
    tokens, width = x_ref.shape
    here, there = (iota((tokens, tokens), 0), iota((tokens, tokens), 1))
    col = ids_col[...]
    row = jnp.sum(jnp.where(here == there, col, 0), axis=0, keepdims=True)
    same = col == row
    earlier = jnp.where(same & (there < here), 1.0, 0.0)
    later = jnp.where(same & (here < there), 1.0, 0.0)
    slot_col[...] = col * MOST + jnp.sum(earlier, axis=1, keepdims=True).astype(jnp.int32)
    slot_row[...] = row * MOST + jnp.sum(later, axis=0, keepdims=True).astype(jnp.int32)
    for c, out in enumerate(outs):
        held = slots_of(out, tokens, c, len(outs)) == slot_row[...]
        chosen = jnp.where(held, 1.0, 0.0)
        taken = jnp.sum(chosen, axis=1, keepdims=True)
        value = dot(chosen.astype(jnp.bfloat16), x_ref[...])
        first = iota(value.shape, 1) == 0
        value = value + jnp.where(first & (taken == 0.0), EMPTY, 0.0)
        out[...] = value.astype(jnp.bfloat16).reshape(out.shape)


def place(cluster, x, owners, rows, chunks):
    tokens = x.shape[0]
    piece = jax.ShapeDtypeStruct((owners, rows, x.shape[1]), jnp.bfloat16)
    return pl.pallas_call(
        place_kernel,
        out_shape=(
            jax.ShapeDtypeStruct((tokens, 1), jnp.int32),
            jax.ShapeDtypeStruct((1, tokens), jnp.int32),
        )
        + (piece,) * chunks,
        compiler_params=pltpu.CompilerParams(vmem_limit_bytes=GRANT),
        cost_estimate=cost(1),
        name="place",
    )(cluster, x)


def head_grads_kernel(blk, a0, a1, a2, a3, w_out, slot_row, out_ref):
    width = a0.shape[1]
    total = None
    for j, part in enumerate((a0, a1, a2, a3)):
        cols = pl.ds(pl.multiple_of(blk[j] * width, width), width)
        term = dot(part[...], w_out[:, cols], NT)
        total = term if total is None else total + term
    slots, tokens = (out_ref.shape[0], a0.shape[0])
    chosen = jnp.where(iota((slots, tokens), 0) == slot_row[...], 1.0, 0.0).astype(jnp.bfloat16)
    out_ref[...] = dot(chosen, total.astype(jnp.bfloat16)).astype(jnp.bfloat16)


def head_grads(blk, parts, w_out, slot_row):
    return pl.pallas_call(
        head_grads_kernel,
        out_shape=jax.ShapeDtypeStruct((CLUSTERS * MOST, w_out.shape[0]), jnp.bfloat16),
        in_specs=[SMEM] + [VMEM] * 6,
        out_specs=VMEM,
        compiler_params=pltpu.CompilerParams(vmem_limit_bytes=GRANT),
        cost_estimate=cost(1),
        name="head_grads",
    )(blk, *parts, w_out, slot_row)


GROUP = 16


def spans(blk, width):
    return [pl.ds(pl.multiple_of(blk[j] * width, width), width) for j in range(4)]


def load_all(first, sources, targets, sems):
    @pl.when(first)
    def _():
        for source, target, i in zip(sources, targets, range(3)):
            pltpu.make_async_copy(source, target, sems.at[i]).start()


def wait_for(first, source, target, sem):
    @pl.when(first)
    def _():
        pltpu.make_async_copy(source, target, sem).wait()


def forward_kernel(blk, x0, x1, x2, x3, wq, wk, wv, *refs):
    mixed, saved, probs_ref = refs[-3:]
    sources, rows, width = x0.shape
    heads_width = wq.shape[1]
    heads = heads_width // HEAD_DIM
    scale = HEAD_DIM ** (-0.5)
    span = spans(blk, width)
    members = sources * GROUP
    shape = (sources, GROUP, members)
    here = (iota(shape, 1) // MOST).reshape(members, members)
    source_here = iota(shape, 0).reshape(members, members)
    place_here = iota(shape, 1).reshape(members, members)
    lane = iota((members, members), 1)
    there = lane % GROUP // MOST
    same = here == there
    earlier = same & (lane // GROUP < source_here)
    later = same & (lane // GROUP > source_here)
    diagonal = source_here * GROUP + place_here == lane
    rank_col = (place_here % MOST).astype(jnp.float32)[:, :1]
    rank_row = (lane % MOST).astype(jnp.float32)[:1, :]
    groups = [slice(n * GROUP, (n + 1) * GROUP) for n in range(rows // GROUP)]
    kept, usable = ([], [])
    for group in groups:
        mark = x0[:, group, :HEAD_DIM].reshape(members, HEAD_DIM)[:, :1].astype(jnp.float32)
        held_col = jnp.where(mark <= LIMIT, 1.0, 0.0)
        held_row = jnp.sum(jnp.where(diagonal, held_col, 0.0), axis=0, keepdims=True)
        place_col = rank_col + jnp.sum(jnp.where(earlier, held_row, 0.0), axis=1, keepdims=True)
        place_row = rank_row + jnp.sum(jnp.where(later, held_col, 0.0), axis=0, keepdims=True)
        kept.append(jnp.where(place_col < CAP, held_col, 0.0))
        usable.append(same & (jnp.where(place_row < CAP, held_row, 0.0) > 0))

    xs = [r[...].reshape(sources * rows, width) for r in (x0, x1, x2, x3)]
    for i, w in enumerate((wq, wk, wv)):
        total = dot(xs[0], w[span[0], :])
        for j in range(1, 4):
            total = total + dot(xs[j], w[span[j], :])
        saved[:, :, i * heads_width : (i + 1) * heads_width] = total.astype(jnp.bfloat16).reshape(
            sources, rows, heads_width
        )

    def part(i, n, h):
        start = i * heads_width + h * HEAD_DIM
        return saved[:, groups[n], start : start + HEAD_DIM].reshape(members, HEAD_DIM)

    every = [(n, h) for n in range(len(groups)) for h in range(heads)]
    scores = [
        jnp.where(usable[n], dot(part(0, n, h), part(1, n, h), NT) * scale, -1e30)
        for n, h in every
    ]
    raised = [jnp.exp(s - jnp.max(s, axis=1, keepdims=True)) for s in scores]
    probs = [
        r * (kept[n] / jnp.sum(r, axis=1, keepdims=True)) for (n, h), r in zip(every, raised)
    ]
    for (n, h), p in zip(every, probs):
        probs_ref[0, n, h] = p
        out = dot(p.astype(jnp.bfloat16), part(2, n, h)).astype(jnp.bfloat16)
        mixed[:, groups[n], h * HEAD_DIM : (h + 1) * HEAD_DIM] = out.reshape(
            sources, GROUP, HEAD_DIM
        )


def backward_kernel(blk, saved, probs_ref, g_ref, wq, wk, wv, *refs):
    keep, give, (dq, dk, dv) = (refs[:2], refs[2:6], refs[6:])
    sources, rows, _ = saved.shape
    width = keep[0].shape[2]
    heads_width = wq.shape[1]
    heads = heads_width // HEAD_DIM
    scale = HEAD_DIM ** (-0.5)
    span = spans(blk, width)
    members = sources * GROUP
    groups = [slice(n * GROUP, (n + 1) * GROUP) for n in range(rows // GROUP)]
    every = [(n, h) for n in range(len(groups)) for h in range(heads)]

    def part(i, n, h):
        start = i * heads_width + h * HEAD_DIM
        return saved[:, groups[n], start : start + HEAD_DIM].reshape(members, HEAD_DIM)

    def grad(n, h):
        return g_ref[:, groups[n], h * HEAD_DIM : (h + 1) * HEAD_DIM].reshape(members, HEAD_DIM)

    def put(ref, n, h, value):
        cols = slice(h * HEAD_DIM, (h + 1) * HEAD_DIM)
        ref[:, groups[n], cols] = value.astype(jnp.bfloat16).reshape(sources, GROUP, HEAD_DIM)

    grad_probs = [dot(grad(n, h), part(2, n, h), NT) for n, h in every]
    for n, h in every:
        put(dv, n, h, dot(probs_ref[0, n, h].astype(jnp.bfloat16), grad(n, h), TN))
    inner = [
        jnp.sum(gp * probs_ref[0, n, h], axis=1, keepdims=True)
        for (n, h), gp in zip(every, grad_probs)
    ]
    grad_scores = [
        (probs_ref[0, n, h] * (gp - i) * scale).astype(jnp.bfloat16)
        for (n, h), gp, i in zip(every, grad_probs, inner)
    ]
    for (n, h), gs in zip(every, grad_scores):
        put(dq, n, h, dot(gs, part(1, n, h)))
    for (n, h), gs in zip(every, grad_scores):
        put(dk, n, h, dot(gs, part(0, n, h), TN))
    grads = [d[...].reshape(sources * rows, heads_width) for d in (dq, dk, dv)]
    for j in (1, 3, 0, 2):
        total = None
        for d, w in zip(grads, (wq, wk, wv)):
            term = dot(d, w[span[j], :], NT)
            total = term if total is None else total + term
        total = total.astype(jnp.bfloat16).reshape(sources, rows, width)
        if j % 2 == 0:
            keep[j // 2][...] = total
        else:
            give[j - 1][...] = total[: sources // 2]
            give[j][...] = total[sources // 2 :]


def step_of(sources, rows):
    step = GROUP
    while step * 2 * sources <= 256 and rows % (step * 2) == 0:
        step *= 2
    return step


def forward(blk, parts, wq, wk, wv, chunk, chunks, mixed):
    sources, rows, width = parts[2].shape
    heads_width = wq.shape[1]
    heads = heads_width // HEAD_DIM
    step = step_of(sources, rows)
    steps, groups, members = (rows // step, step // GROUP, sources * GROUP)
    block = pl.BlockSpec((sources, step, width), lambda p: (0, p, 0))
    weight = VMEM
    in_specs = [SMEM] + [block] * 4 + [weight] * 3
    operands = [blk, *parts, wq, wk, wv]
    if mixed is not None:
        in_specs.append(pl.BlockSpec(memory_space=pl.ANY))
        operands.append(mixed)
    return pl.pallas_call(
        forward_kernel,
        grid=(steps,),
        out_shape=(
            jax.ShapeDtypeStruct((sources, rows * chunks, heads_width), jnp.bfloat16),
            jax.ShapeDtypeStruct((sources, rows, 3 * heads_width), jnp.bfloat16),
            jax.ShapeDtypeStruct((steps, groups, heads, members, members), jnp.float32),
        ),
        in_specs=in_specs,
        out_specs=(
            pl.BlockSpec((sources, step, heads_width), lambda p: (0, p + chunk * steps, 0)),
            pl.BlockSpec((sources, step, 3 * heads_width), lambda p: (0, p, 0)),
            pl.BlockSpec((1, groups, heads, members, members), lambda p: (p, 0, 0, 0, 0)),
        ),
        input_output_aliases={} if mixed is None else {len(operands) - 1: 0},
        compiler_params=pltpu.CompilerParams(vmem_limit_bytes=40 * MB),
        cost_estimate=cost(1),
        name="forward",
    )(*operands)


def backward(blk, saved, probs, grads, wq, wk, wv, chunk):
    sources, rows, _ = saved.shape
    heads_width = wq.shape[1]
    width = wq.shape[0] // 4
    heads = heads_width // HEAD_DIM
    step = step_of(sources, rows)
    steps, groups, members = (rows // step, step // GROUP, sources * GROUP)
    block = pl.BlockSpec((sources, step, width), lambda p: (0, p, 0))
    half = pl.BlockSpec((sources // 2, step, width), lambda p: (0, p, 0))
    weight = VMEM
    shape = jax.ShapeDtypeStruct((sources, rows, width), jnp.bfloat16)
    half_shape = jax.ShapeDtypeStruct((sources // 2, rows, width), jnp.bfloat16)
    outs = pl.pallas_call(
        backward_kernel,
        grid=(steps,),
        out_shape=(shape,) * 2 + (half_shape,) * 4,
        in_specs=[
            SMEM,
            pl.BlockSpec((sources, step, 3 * heads_width), lambda p: (0, p, 0)),
            pl.BlockSpec((1, groups, heads, members, members), lambda p: (p, 0, 0, 0, 0)),
            pl.BlockSpec((sources, step, heads_width), lambda p: (0, p + chunk * steps, 0)),
            weight,
            weight,
            weight,
        ],
        out_specs=(block,) * 2 + (half,) * 4,
        scratch_shapes=[pltpu.VMEM((sources, step, heads_width), jnp.bfloat16)] * 3,
        compiler_params=pltpu.CompilerParams(vmem_limit_bytes=50 * MB),
        cost_estimate=cost(1),
        name="backward",
    )(blk, saved, probs, grads, wq, wk, wv)
    return (outs[:2], outs[2:])


def slab(w, blk, j):
    width = w.shape[0] // 4
    return lax.dynamic_slice_in_dim(w, blk[j] * width, width, 0)


def by_cluster(x):
    sources, rows = x.shape[:2]
    x = x.reshape(sources, rows // MOST, MOST, -1).transpose(1, 0, 2, 3)
    return x.reshape(rows // MOST, sources * MOST, -1)


def by_source(x, sources):
    clusters = x.shape[0]
    x = x.reshape(clusters, sources, MOST, -1).transpose(1, 0, 2, 3)
    return x.reshape(sources, clusters * MOST, -1)


def split_heads(x):
    return x.reshape(x.shape[0], -1, HEAD_DIM)


ein = functools.partial(jnp.einsum, preferred_element_type=jnp.float32)


def forward_many(blk, parts, wq, wk, wv):
    sources, rows, _ = parts[0].shape

    def project(w):
        total = 0.0
        for j in range(4):
            total = total + ein("srd,dh->srh", parts[j], slab(w, blk, j))
        return by_cluster(total.astype(jnp.bfloat16))

    held = (parts[0][:, :, 0].astype(jnp.float32) <= LIMIT).reshape(sources, -1, MOST)
    counts = jnp.sum(held.astype(jnp.int32), axis=2, keepdims=True)
    rank = jnp.cumsum(counts, axis=0) - counts + jnp.arange(MOST)
    kept = by_cluster((held & (rank < CAP)).astype(jnp.float32).reshape(sources, rows, 1))
    scale = HEAD_DIM ** (-0.5)

    def one(args):
        q, k, v, live = args
        q, k, v = (split_heads(a) for a in (q, k, v))
        scores = jnp.where(live[None, None, :, 0] > 0, ein("qhd,khd->hqk", q, k) * scale, -1e30)
        raised = jnp.exp(scores - jnp.max(scores, axis=-1, keepdims=True))
        probs = raised * (live / jnp.sum(raised, axis=-1, keepdims=True))
        mixed = ein("hqk,khd->qhd", probs.astype(jnp.bfloat16), v).astype(jnp.bfloat16)
        return (mixed.reshape(mixed.shape[0], -1), probs)

    saved = tuple(project(w) for w in (wq, wk, wv))
    mixed, probs = lax.map(one, saved + (kept,))
    return (by_source(mixed, sources), saved, probs)


def backward_many(blk, saved, probs, grads, wq, wk, wv):
    sources = grads.shape[0]
    scale = HEAD_DIM ** (-0.5)

    def one(args):
        q, k, v, probs, g = args
        q, k, v, g = (split_heads(a) for a in (q, k, v, g))
        dv = ein("hqk,qhd->khd", probs.astype(jnp.bfloat16), g)
        grad_probs = ein("qhd,khd->hqk", g, v)
        inner = jnp.sum(grad_probs * probs, axis=-1, keepdims=True)
        grad_scores = (probs * (grad_probs - inner) * scale).astype(jnp.bfloat16)
        dq = ein("hqk,khd->qhd", grad_scores, k)
        dk = ein("hqk,qhd->khd", grad_scores, q)
        return tuple(a.astype(jnp.bfloat16).reshape(a.shape[0], -1) for a in (dq, dk, dv))

    dq, dk, dv = lax.map(one, saved + (probs, by_cluster(grads)))
    outs = []
    for j in range(4):
        total = 0.0
        for d, w in ((dq, wq), (dk, wk), (dv, wv)):
            total = total + ein("crh,wh->crw", d, slab(w, blk, j))
        outs.append(by_source(total.astype(jnp.bfloat16), sources))
    half = sources // 2
    return ((outs[0], outs[2]), (outs[1][:half], outs[1][half:], outs[3][:half], outs[3][half:]))


def pick(slot_col, parts):
    total = None
    for c, part in enumerate(parts):
        owners, rows, width = part.shape
        i = iota((1, owners * rows), 1)
        slots = i // rows * (rows * len(parts)) + i % rows + c * rows
        chosen = jnp.where(slots == slot_col[...], 1.0, 0.0).astype(jnp.bfloat16)
        term = dot(chosen, part[...].reshape(owners * rows, width))
        total = term if total is None else total + term
    return total


def out_kernel(blk, slot_col, w_out, mixed, *outs):
    keep, give = (outs[:2], outs[2:])
    heads = pick(slot_col, (mixed,)).astype(jnp.bfloat16)
    tokens, width = keep[0].shape
    span = spans(blk, width)
    for j in (1, 3, 0, 2):
        total = dot(heads, w_out[:, span[j]]).astype(jnp.bfloat16)
        if j % 2 == 0:
            keep[j // 2][...] = total
        else:
            give[j - 1][...] = total[: tokens // 2]
            give[j][...] = total[tokens // 2 :]


def project_out(blk, slot_col, w_out, mixed):
    tokens, width = (slot_col.shape[0], w_out.shape[1] // 4)
    shape = jax.ShapeDtypeStruct((tokens, width), jnp.bfloat16)
    half = jax.ShapeDtypeStruct((tokens // 2, width), jnp.bfloat16)
    outs = pl.pallas_call(
        out_kernel,
        out_shape=(shape,) * 2 + (half,) * 4,
        in_specs=[SMEM] + [VMEM] * 3,
        out_specs=(VMEM,) * 6,
        compiler_params=pltpu.CompilerParams(vmem_limit_bytes=GRANT),
        cost_estimate=cost(1),
        name="project_out",
    )(blk, slot_col, w_out, mixed)
    return (outs[:2], outs[2:])


def final_kernel(slot_col, *refs):
    refs[-1][...] = pick(slot_col, refs[:-1])


def to_tokens(slot_col, parts):
    return pl.pallas_call(
        final_kernel,
        out_shape=jax.ShapeDtypeStruct((slot_col.shape[0], parts[0].shape[2]), jnp.float32),
        compiler_params=pltpu.CompilerParams(vmem_limit_bytes=GRANT),
        cost_estimate=cost(1),
        name="to_tokens",
    )(slot_col, *parts)


def wide(x):
    return x.astype(jnp.float32)


def add_kernel(*refs):
    whole, halves, more, out = (refs[0], refs[1:3], refs[3:-1], refs[-1])
    size = whole.shape[0] // 2
    for i, half in enumerate(halves):
        rows = slice(i * size, (i + 1) * size)
        total = wide(whole[rows]) + wide(half[...])
        if more:
            total = total + wide(more[0][rows])
        out[rows] = total.astype(jnp.bfloat16)


def add(whole, first, second, *more, into=None, chunk=0, chunks=1):
    shape = whole.shape
    block = pl.BlockSpec(shape, lambda p: (0,) * len(shape))
    half = pl.BlockSpec(first.shape, lambda p: (0,) * len(shape))
    place = (0, chunk, 0)[: len(shape)]
    full = (shape[0], shape[1] * chunks) + shape[2:] if chunks > 1 else shape
    operands = [whole, first, second, *more]
    in_specs = [block, half, half] + [block] * len(more)
    kernel, aliases = (add_kernel, {})
    if into is not None:
        aliases = {len(operands): 0}
        operands.append(into)
        in_specs.append(pl.BlockSpec(memory_space=pl.ANY))

        def kernel(*refs):
            add_kernel(*refs[:-2], refs[-1])

    return pl.pallas_call(
        kernel,
        grid=(1,),
        out_shape=jax.ShapeDtypeStruct(full, jnp.bfloat16),
        in_specs=in_specs,
        out_specs=pl.BlockSpec(shape, lambda p: place if chunks > 1 else (0,) * len(shape)),
        input_output_aliases=aliases,
        compiler_params=pltpu.CompilerParams(vmem_limit_bytes=GRANT),
        cost_estimate=cost(0.001),
        name="add",
    )(*operands)


def reduce_pairs(keep, give):
    got = [swap(x, 1) for x in give]
    return (keep[0], got[:2], add(keep[1], *got[2:]))


def body(normed, cluster, w_query, w_key, w_value, w_out, grad_out):
    seq_count = lax.axis_size("seq")
    per = CLUSTERS // seq_count * MOST
    chunks = CHUNKS if per // CHUNKS % GROUP == 0 else 1
    rows = per // chunks
    blk = lax.axis_index("tp") ^ jnp.arange(4, dtype=jnp.int32)
    weights = (w_query, w_key, w_value)
    small = seq_count * GROUP <= 256

    g_across = swap(grad_out, 2)
    g_parts = (grad_out, swap(grad_out, 1), g_across, swap(g_across, 1))
    slot_col, slot_row, *pieces = place(cluster, normed, seq_count, rows, chunks)
    xs, x_across = ([], [])
    for piece in pieces:
        xs.append(exchange(after(piece, *xs[-1:])))
    for x in xs:
        x_across.append(swap(x, 2))
    g_slots = head_grads(blk, g_parts, w_out, slot_row).reshape(seq_count, per, -1)
    g = exchange(after(g_slots, xs[-1], x_across[0]))

    mixed, saved = (None, [])
    for c in range(chunks):
        if c > 0:
            x_across[c] = after(x_across[c], mixed)
        parts = (xs[c], swap(xs[c], 1), x_across[c], swap(x_across[c], 1))
        if small:
            mixed, *kept = forward(blk, parts, *weights, c, chunks, mixed)
        else:
            mixed, *kept = forward_many(blk, parts, *weights)
        saved.append(kept)
    mixed_back = exchange(after(mixed, g))

    g = after(g, mixed)
    for c in range(chunks):
        if small:
            keep, give = backward(blk, *saved[c], g, *weights, c)
        else:
            keep, give = backward_many(blk, *saved[c], g, *weights)
        keep, got, partial = reduce_pairs(keep, give)
        g = after(g, partial)
        before_last = partial
        if c > 0:
            partial = after(partial, saved[c - 1][3])
        saved[c] = (keep, *got, swap(partial, 2))
    back, last = ([], mixed_back)
    for c in range(chunks):
        last = exchange(after(add(*saved[c]), last, before_last))
        back.append(last)
        if c == 0:
            keep, give = project_out(blk, slot_col, w_out, mixed_back)
            keep, got, before_last = reduce_pairs(keep, give)
            attended = add(keep, *got, swap(before_last, 2))
    return (attended, to_tokens(slot_col, back))


def solution(mesh):
    in_specs = (
        P("seq", "tp"),
        P("seq", None),
        P(None, "tp"),
        P(None, "tp"),
        P(None, "tp"),
        P("tp", None),
        P("seq", "tp"),
    )
    out_specs = (P("seq", "tp"), P("seq", "tp"))
    return jax.shard_map(body, mesh=mesh, in_specs=in_specs, out_specs=out_specs, check_vma=False)
```

```python
import functools
import jax
import jax.numpy as jnp
from jax import lax
from jax.experimental import pallas as pl
from jax.experimental.pallas import tpu as pltpu
from jax.sharding import PartitionSpec as P

HEAD_DIM = 128
CLUSTERS = 128
CAP = 256
MOST = 8
LIMIT = 24.0
EMPTY = 32.0
NN = (((1,), (0,)), ((), ()))
NT = (((1,), (1,)), ((), ()))
TN = (((0,), (0,)), ((), ()))
MB = 1024 * 1024
CHUNKS = 2
GRANT = 50 * MB


def cost(giga):
    return pl.CostEstimate(flops=int(giga * 1e9), bytes_accessed=MB, transcendentals=0)


VMEM = pl.BlockSpec(memory_space=pltpu.VMEM)
SMEM = pl.BlockSpec(memory_space=pltpu.SMEM)


def dot(a, b, dims=NN):
    return lax.dot_general(a, b, dims, preferred_element_type=jnp.float32)


def iota(shape, dim):
    return lax.broadcasted_iota(jnp.int32, shape, dim)


def swap(x, bit):
    count = lax.axis_size("tp")
    return lax.ppermute(x, "tp", [(i, i ^ bit) for i in range(count)])


def exchange(x):
    return lax.all_to_all(x, "seq", split_axis=0, concat_axis=0, tiled=True)


def after(x, *others):
    return lax.optimization_barrier((x,) + others)[0]


def slots_of(out, tokens, chunk, chunks):
    owners, rows, _ = out.shape
    shape = (owners, rows, tokens)
    slot = iota(shape, 0) * (rows * chunks) + iota(shape, 1) + chunk * rows
    return slot.reshape(owners * rows, tokens)


def put_rows(slot_row, x_ref, out, chunk, chunks):
    tokens = x_ref.shape[0]
    held = slots_of(out, tokens, chunk, chunks) == slot_row
    chosen = jnp.where(held, 1.0, 0.0)
    taken = jnp.sum(chosen, axis=1, keepdims=True)
    value = dot(chosen.astype(jnp.bfloat16), x_ref[...])
    first = iota(value.shape, 1) == 0
    value = value + jnp.where(first & (taken == 0.0), EMPTY, 0.0)
    out[...] = value.astype(jnp.bfloat16).reshape(out.shape)


def place_kernel(chunks, ids_row, x_ref, slot_col, slot_row, out):
    tokens = x_ref.shape[0]
    here, there = (iota((tokens, tokens), 0), iota((tokens, tokens), 1))
    row = ids_row[...]
    col = jnp.sum(jnp.where(here == there, row, 0), axis=1, keepdims=True)
    same = col == row
    earlier = jnp.where(same & (there < here), 1.0, 0.0)
    later = jnp.where(same & (here < there), 1.0, 0.0)
    slot_col[...] = col * MOST + jnp.sum(earlier, axis=1, keepdims=True).astype(jnp.int32)
    rows = row * MOST + jnp.sum(later, axis=0, keepdims=True).astype(jnp.int32)
    slot_row[...] = rows
    put_rows(rows, x_ref, out, 0, chunks)


def place_more_kernel(chunk, chunks, slot_row, x_ref, out):
    put_rows(slot_row[...], x_ref, out, chunk, chunks)


def place(ids_row, x, owners, rows, chunks):
    tokens = x.shape[0]
    piece = jax.ShapeDtypeStruct((owners, rows, x.shape[1]), jnp.bfloat16)
    options = dict(
        compiler_params=pltpu.CompilerParams(vmem_limit_bytes=60 * MB), cost_estimate=cost(1)
    )
    slot_col, slot_row, first = pl.pallas_call(
        functools.partial(place_kernel, chunks),
        out_shape=(
            jax.ShapeDtypeStruct((tokens, 1), jnp.int32),
            jax.ShapeDtypeStruct((1, tokens), jnp.int32),
            piece,
        ),
        name="place",
        **options,
    )(ids_row, x)
    pieces = [first]
    for c in range(1, chunks):
        kernel = functools.partial(place_more_kernel, c, chunks)
        more = pl.pallas_call(kernel, out_shape=piece, name="place_more", **options)
        pieces.append(more(slot_row, x))
    return (slot_col, slot_row, *pieces)


def head_grads_kernel(blk, a0, a1, a2, a3, w_out, slot_row, out_ref):
    width = a0.shape[1]
    total = None
    for j, part in enumerate((a0, a1, a2, a3)):
        cols = pl.ds(pl.multiple_of(blk[j] * width, width), width)
        term = dot(part[...], w_out[:, cols], NT)
        total = term if total is None else total + term
    slots, tokens = (out_ref.shape[0], a0.shape[0])
    chosen = jnp.where(iota((slots, tokens), 0) == slot_row[...], 1.0, 0.0).astype(jnp.bfloat16)
    out_ref[...] = dot(chosen, total.astype(jnp.bfloat16)).astype(jnp.bfloat16)


def head_grads(blk, parts, w_out, slot_row):
    return pl.pallas_call(
        head_grads_kernel,
        out_shape=jax.ShapeDtypeStruct((CLUSTERS * MOST, w_out.shape[0]), jnp.bfloat16),
        in_specs=[SMEM] + [VMEM] * 6,
        out_specs=VMEM,
        compiler_params=pltpu.CompilerParams(vmem_limit_bytes=GRANT),
        cost_estimate=cost(2),
        name="head_grads",
    )(blk, *parts, w_out, slot_row)


GROUP = 16


def spans(blk, width):
    return [pl.ds(pl.multiple_of(blk[j] * width, width), width) for j in range(4)]


def load_all(first, sources, targets, sems):
    @pl.when(first)
    def _():
        for source, target, i in zip(sources, targets, range(3)):
            pltpu.make_async_copy(source, target, sems.at[i]).start()


def wait_for(first, source, target, sem):
    @pl.when(first)
    def _():
        pltpu.make_async_copy(source, target, sem).wait()


def forward_kernel(blk, x0, x1, x2, x3, wq, wk, wv, *refs):
    mixed, saved, probs_ref = refs[-3:]
    sources, rows, width = x0.shape
    heads_width = wq.shape[1]
    heads = heads_width // HEAD_DIM
    scale = HEAD_DIM ** (-0.5)
    span = spans(blk, width)
    members = sources * GROUP
    shape = (sources, GROUP, members)
    here = (iota(shape, 1) // MOST).reshape(members, members)
    source_here = iota(shape, 0).reshape(members, members)
    place_here = iota(shape, 1).reshape(members, members)
    lane = iota((members, members), 1)
    there = lane % GROUP // MOST
    same = here == there
    earlier = same & (lane // GROUP < source_here)
    later = same & (lane // GROUP > source_here)
    diagonal = source_here * GROUP + place_here == lane
    rank_col = (place_here % MOST).astype(jnp.float32)[:, :1]
    rank_row = (lane % MOST).astype(jnp.float32)[:1, :]
    groups = [slice(n * GROUP, (n + 1) * GROUP) for n in range(rows // GROUP)]
    kept, usable = ([], [])
    for group in groups:
        mark = x0[:, group, :HEAD_DIM].reshape(members, HEAD_DIM)[:, :1].astype(jnp.float32)
        held_col = jnp.where(mark <= LIMIT, 1.0, 0.0)
        held_row = jnp.sum(jnp.where(diagonal, held_col, 0.0), axis=0, keepdims=True)
        place_col = rank_col + jnp.sum(jnp.where(earlier, held_row, 0.0), axis=1, keepdims=True)
        place_row = rank_row + jnp.sum(jnp.where(later, held_col, 0.0), axis=0, keepdims=True)
        kept.append(jnp.where(place_col < CAP, held_col, 0.0))
        usable.append(same & (jnp.where(place_row < CAP, held_row, 0.0) > 0))

    xs = [r[...].reshape(sources * rows, width) for r in (x0, x1, x2, x3)]
    for i, w in enumerate((wq, wk, wv)):
        total = dot(xs[0], w[span[0], :])
        for j in range(1, 4):
            total = total + dot(xs[j], w[span[j], :])
        saved[:, :, i * heads_width : (i + 1) * heads_width] = total.astype(jnp.bfloat16).reshape(
            sources, rows, heads_width
        )

    def part(i, n, h):
        start = i * heads_width + h * HEAD_DIM
        return saved[:, groups[n], start : start + HEAD_DIM].reshape(members, HEAD_DIM)

    every = [(n, h) for n in range(len(groups)) for h in range(heads)]
    scores = [
        jnp.where(usable[n], dot(part(0, n, h), part(1, n, h), NT) * scale, -1e30)
        for n, h in every
    ]
    raised = [jnp.exp(s - jnp.max(s, axis=1, keepdims=True)) for s in scores]
    probs = [
        r * (kept[n] / jnp.sum(r, axis=1, keepdims=True)) for (n, h), r in zip(every, raised)
    ]
    for (n, h), p in zip(every, probs):
        probs_ref[0, n, h] = p
        out = dot(p.astype(jnp.bfloat16), part(2, n, h)).astype(jnp.bfloat16)
        mixed[:, groups[n], h * HEAD_DIM : (h + 1) * HEAD_DIM] = out.reshape(
            sources, GROUP, HEAD_DIM
        )


def backward_kernel(blk, saved, probs_ref, g_ref, wq, wk, wv, *refs):
    keep, give, (dq, dk, dv) = (refs[:2], refs[2:6], refs[6:])
    sources, rows, _ = saved.shape
    width = keep[0].shape[2]
    heads_width = wq.shape[1]
    heads = heads_width // HEAD_DIM
    scale = HEAD_DIM ** (-0.5)
    span = spans(blk, width)
    members = sources * GROUP
    groups = [slice(n * GROUP, (n + 1) * GROUP) for n in range(rows // GROUP)]
    every = [(n, h) for n in range(len(groups)) for h in range(heads)]

    def part(i, n, h):
        start = i * heads_width + h * HEAD_DIM
        return saved[:, groups[n], start : start + HEAD_DIM].reshape(members, HEAD_DIM)

    def grad(n, h):
        return g_ref[:, groups[n], h * HEAD_DIM : (h + 1) * HEAD_DIM].reshape(members, HEAD_DIM)

    def put(ref, n, h, value):
        cols = slice(h * HEAD_DIM, (h + 1) * HEAD_DIM)
        ref[:, groups[n], cols] = value.astype(jnp.bfloat16).reshape(sources, GROUP, HEAD_DIM)

    grad_probs = [dot(grad(n, h), part(2, n, h), NT) for n, h in every]
    for n, h in every:
        put(dv, n, h, dot(probs_ref[0, n, h].astype(jnp.bfloat16), grad(n, h), TN))
    inner = [
        jnp.sum(gp * probs_ref[0, n, h], axis=1, keepdims=True)
        for (n, h), gp in zip(every, grad_probs)
    ]
    grad_scores = [
        (probs_ref[0, n, h] * (gp - i) * scale).astype(jnp.bfloat16)
        for (n, h), gp, i in zip(every, grad_probs, inner)
    ]
    for (n, h), gs in zip(every, grad_scores):
        put(dq, n, h, dot(gs, part(1, n, h)))
    for (n, h), gs in zip(every, grad_scores):
        put(dk, n, h, dot(gs, part(0, n, h), TN))
    grads = [d[...].reshape(sources * rows, heads_width) for d in (dq, dk, dv)]
    for j in (1, 3, 0, 2):
        total = None
        for d, w in zip(grads, (wq, wk, wv)):
            term = dot(d, w[span[j], :], NT)
            total = term if total is None else total + term
        total = total.astype(jnp.bfloat16).reshape(sources, rows, width)
        if j % 2 == 0:
            keep[j // 2][...] = total
        else:
            give[j - 1][...] = total[: sources // 2]
            give[j][...] = total[sources // 2 :]


def step_of(sources, rows):
    step = GROUP
    while step * 2 * sources <= 256 and rows % (step * 2) == 0:
        step *= 2
    return step


def forward(blk, parts, wq, wk, wv, chunk, chunks, mixed):
    sources, rows, width = parts[2].shape
    heads_width = wq.shape[1]
    heads = heads_width // HEAD_DIM
    step = step_of(sources, rows)
    steps, groups, members = (rows // step, step // GROUP, sources * GROUP)
    block = pl.BlockSpec((sources, step, width), lambda p: (0, p, 0))
    weight = VMEM
    in_specs = [SMEM] + [block] * 4 + [weight] * 3
    operands = [blk, *parts, wq, wk, wv]
    if mixed is not None:
        in_specs.append(pl.BlockSpec(memory_space=pl.ANY))
        operands.append(mixed)
    return pl.pallas_call(
        forward_kernel,
        grid=(steps,),
        out_shape=(
            jax.ShapeDtypeStruct((sources, rows * chunks, heads_width), jnp.bfloat16),
            jax.ShapeDtypeStruct((sources, rows, 3 * heads_width), jnp.bfloat16),
            jax.ShapeDtypeStruct((steps, groups, heads, members, members), jnp.float32),
        ),
        in_specs=in_specs,
        out_specs=(
            pl.BlockSpec((sources, step, heads_width), lambda p: (0, p + chunk * steps, 0)),
            pl.BlockSpec((sources, step, 3 * heads_width), lambda p: (0, p, 0)),
            pl.BlockSpec((1, groups, heads, members, members), lambda p: (p, 0, 0, 0, 0)),
        ),
        input_output_aliases={} if mixed is None else {len(operands) - 1: 0},
        compiler_params=pltpu.CompilerParams(vmem_limit_bytes=40 * MB),
        cost_estimate=cost(2),
        name="forward",
    )(*operands)


def backward(blk, saved, probs, grads, wq, wk, wv, chunk):
    sources, rows, _ = saved.shape
    heads_width = wq.shape[1]
    width = wq.shape[0] // 4
    heads = heads_width // HEAD_DIM
    step = step_of(sources, rows)
    steps, groups, members = (rows // step, step // GROUP, sources * GROUP)
    block = pl.BlockSpec((sources, step, width), lambda p: (0, p, 0))
    half = pl.BlockSpec((sources // 2, step, width), lambda p: (0, p, 0))
    weight = VMEM
    shape = jax.ShapeDtypeStruct((sources, rows, width), jnp.bfloat16)
    half_shape = jax.ShapeDtypeStruct((sources // 2, rows, width), jnp.bfloat16)
    outs = pl.pallas_call(
        backward_kernel,
        grid=(steps,),
        out_shape=(shape,) * 2 + (half_shape,) * 4,
        in_specs=[
            SMEM,
            pl.BlockSpec((sources, step, 3 * heads_width), lambda p: (0, p, 0)),
            pl.BlockSpec((1, groups, heads, members, members), lambda p: (p, 0, 0, 0, 0)),
            pl.BlockSpec((sources, step, heads_width), lambda p: (0, p + chunk * steps, 0)),
            weight,
            weight,
            weight,
        ],
        out_specs=(block,) * 2 + (half,) * 4,
        scratch_shapes=[pltpu.VMEM((sources, step, heads_width), jnp.bfloat16)] * 3,
        compiler_params=pltpu.CompilerParams(vmem_limit_bytes=GRANT),
        cost_estimate=cost(2),
        name="backward",
    )(blk, saved, probs, grads, wq, wk, wv)
    return (outs[:2], outs[2:])


def slab(w, blk, j):
    width = w.shape[0] // 4
    return lax.dynamic_slice_in_dim(w, blk[j] * width, width, 0)


def by_cluster(x):
    sources, rows = x.shape[:2]
    x = x.reshape(sources, rows // MOST, MOST, -1).transpose(1, 0, 2, 3)
    return x.reshape(rows // MOST, sources * MOST, -1)


def by_source(x, sources):
    clusters = x.shape[0]
    x = x.reshape(clusters, sources, MOST, -1).transpose(1, 0, 2, 3)
    return x.reshape(sources, clusters * MOST, -1)


def split_heads(x):
    return x.reshape(x.shape[0], -1, HEAD_DIM)


ein = functools.partial(jnp.einsum, preferred_element_type=jnp.float32)


def forward_many(blk, parts, wq, wk, wv):
    sources, rows, _ = parts[0].shape

    def project(w):
        total = 0.0
        for j in range(4):
            total = total + ein("srd,dh->srh", parts[j], slab(w, blk, j))
        return by_cluster(total.astype(jnp.bfloat16))

    held = (parts[0][:, :, 0].astype(jnp.float32) <= LIMIT).reshape(sources, -1, MOST)
    counts = jnp.sum(held.astype(jnp.int32), axis=2, keepdims=True)
    rank = jnp.cumsum(counts, axis=0) - counts + jnp.arange(MOST)
    kept = by_cluster((held & (rank < CAP)).astype(jnp.float32).reshape(sources, rows, 1))
    scale = HEAD_DIM ** (-0.5)

    def one(args):
        q, k, v, live = args
        q, k, v = (split_heads(a) for a in (q, k, v))
        scores = jnp.where(live[None, None, :, 0] > 0, ein("qhd,khd->hqk", q, k) * scale, -1e30)
        raised = jnp.exp(scores - jnp.max(scores, axis=-1, keepdims=True))
        probs = raised * (live / jnp.sum(raised, axis=-1, keepdims=True))
        mixed = ein("hqk,khd->qhd", probs.astype(jnp.bfloat16), v).astype(jnp.bfloat16)
        return (mixed.reshape(mixed.shape[0], -1), probs)

    saved = tuple(project(w) for w in (wq, wk, wv))
    mixed, probs = lax.map(one, saved + (kept,))
    return (by_source(mixed, sources), saved, probs)


def backward_many(blk, saved, probs, grads, wq, wk, wv):
    sources = grads.shape[0]
    scale = HEAD_DIM ** (-0.5)

    def one(args):
        q, k, v, probs, g = args
        q, k, v, g = (split_heads(a) for a in (q, k, v, g))
        dv = ein("hqk,qhd->khd", probs.astype(jnp.bfloat16), g)
        grad_probs = ein("qhd,khd->hqk", g, v)
        inner = jnp.sum(grad_probs * probs, axis=-1, keepdims=True)
        grad_scores = (probs * (grad_probs - inner) * scale).astype(jnp.bfloat16)
        dq = ein("hqk,khd->qhd", grad_scores, k)
        dk = ein("hqk,qhd->khd", grad_scores, q)
        return tuple(a.astype(jnp.bfloat16).reshape(a.shape[0], -1) for a in (dq, dk, dv))

    dq, dk, dv = lax.map(one, saved + (probs, by_cluster(grads)))
    outs = []
    for j in range(4):
        total = 0.0
        for d, w in ((dq, wq), (dk, wk), (dv, wv)):
            total = total + ein("crh,wh->crw", d, slab(w, blk, j))
        outs.append(by_source(total.astype(jnp.bfloat16), sources))
    half = sources // 2
    return ((outs[0], outs[2]), (outs[1][:half], outs[1][half:], outs[3][:half], outs[3][half:]))


def pick(slot_col, parts):
    total = None
    for c, part in enumerate(parts):
        owners, rows, width = part.shape
        i = iota((1, owners * rows), 1)
        slots = i // rows * (rows * len(parts)) + i % rows + c * rows
        chosen = jnp.where(slots == slot_col[...], 1.0, 0.0).astype(jnp.bfloat16)
        term = dot(chosen, part[...].reshape(owners * rows, width))
        total = term if total is None else total + term
    return total


def out_kernel(blk, slot_col, w_out, mixed, *outs):
    keep, give = (outs[:2], outs[2:])
    heads = pick(slot_col, (mixed,)).astype(jnp.bfloat16)
    tokens, width = keep[0].shape
    span = spans(blk, width)
    for j in (1, 3, 0, 2):
        total = dot(heads, w_out[:, span[j]]).astype(jnp.bfloat16)
        if j % 2 == 0:
            keep[j // 2][...] = total
        else:
            give[j - 1][...] = total[: tokens // 2]
            give[j][...] = total[tokens // 2 :]


def project_out(blk, slot_col, w_out, mixed):
    tokens, width = (slot_col.shape[0], w_out.shape[1] // 4)
    shape = jax.ShapeDtypeStruct((tokens, width), jnp.bfloat16)
    half = jax.ShapeDtypeStruct((tokens // 2, width), jnp.bfloat16)
    outs = pl.pallas_call(
        out_kernel,
        out_shape=(shape,) * 2 + (half,) * 4,
        in_specs=[SMEM] + [VMEM] * 3,
        out_specs=(VMEM,) * 6,
        compiler_params=pltpu.CompilerParams(vmem_limit_bytes=GRANT),
        cost_estimate=cost(2),
        name="project_out",
    )(blk, slot_col, w_out, mixed)
    return (outs[:2], outs[2:])


def final_kernel(slot_col, *refs):
    refs[-1][...] = pick(slot_col, refs[:-1])


def to_tokens(slot_col, parts):
    tokens = slot_col.shape[0]
    width = parts[0].shape[2]
    block = tokens
    return pl.pallas_call(
        final_kernel,
        grid=(tokens // block,),
        out_shape=jax.ShapeDtypeStruct((tokens, width), jnp.float32),
        in_specs=[pl.BlockSpec((block, 1), lambda p: (p, 0))]
        + [pl.BlockSpec(parts[0].shape, lambda p: (0, 0, 0))] * len(parts),
        out_specs=pl.BlockSpec((block, width), lambda p: (p, 0)),
        compiler_params=pltpu.CompilerParams(vmem_limit_bytes=GRANT),
        cost_estimate=cost(1),
        name="to_tokens",
    )(slot_col, *parts)


def wide(x):
    return x.astype(jnp.float32)


def add_kernel(*refs):
    whole, halves, more, out = (refs[0], refs[1:3], refs[3:-1], refs[-1])
    size = whole.shape[0] // 2
    for i, half in enumerate(halves):
        rows = slice(i * size, (i + 1) * size)
        total = wide(whole[rows]) + wide(half[...])
        if more:
            total = total + wide(more[0][rows])
        out[rows] = total.astype(jnp.bfloat16)


def add(whole, first, second, *more, into=None, chunk=0, chunks=1):
    shape = whole.shape
    block = pl.BlockSpec(shape, lambda p: (0,) * len(shape))
    half = pl.BlockSpec(first.shape, lambda p: (0,) * len(shape))
    place = (0, chunk, 0)[: len(shape)]
    full = (shape[0], shape[1] * chunks) + shape[2:] if chunks > 1 else shape
    operands = [whole, first, second, *more]
    in_specs = [block, half, half] + [block] * len(more)
    kernel, aliases = (add_kernel, {})
    if into is not None:
        aliases = {len(operands): 0}
        operands.append(into)
        in_specs.append(pl.BlockSpec(memory_space=pl.ANY))

        def kernel(*refs):
            add_kernel(*refs[:-2], refs[-1])

    return pl.pallas_call(
        kernel,
        grid=(1,),
        out_shape=jax.ShapeDtypeStruct(full, jnp.bfloat16),
        in_specs=in_specs,
        out_specs=pl.BlockSpec(shape, lambda p: place if chunks > 1 else (0,) * len(shape)),
        input_output_aliases=aliases,
        compiler_params=pltpu.CompilerParams(vmem_limit_bytes=GRANT),
        cost_estimate=cost(0.001),
        name="add",
    )(*operands)


def reduce_pairs(keep, give):
    got = [swap(x, 1) for x in give]
    return (keep[0], got[:2], add(keep[1], *got[2:]))


def body(normed, cluster, w_query, w_key, w_value, w_out, grad_out):
    seq_count = lax.axis_size("seq")
    per = CLUSTERS // seq_count * MOST
    chunks = CHUNKS if per // CHUNKS % GROUP == 0 else 1
    rows = per // chunks
    blk = lax.axis_index("tp") ^ jnp.arange(4, dtype=jnp.int32)
    weights = (w_query, w_key, w_value)
    small = seq_count * GROUP <= 256

    g_across = swap(grad_out, 2)
    g_parts = (grad_out, swap(grad_out, 1), g_across, swap(g_across, 1))
    slot_col, slot_row, *pieces = place(cluster.reshape(1, -1), normed, seq_count, rows, chunks)
    xs, x_across = ([], [])
    for piece in pieces:
        xs.append(exchange(after(piece, *xs[-1:])))
    for x in xs:
        x_across.append(swap(x, 2))
    g_slots = head_grads(blk, g_parts, w_out, slot_row).reshape(seq_count, per, -1)
    g = exchange(after(g_slots, xs[-1], x_across[0]))

    mixed, saved = (None, [])
    for c in range(chunks):
        if c > 0:
            x_across[c] = after(x_across[c], mixed)
        parts = (xs[c], swap(xs[c], 1), x_across[c], swap(x_across[c], 1))
        if small:
            mixed, *kept = forward(blk, parts, *weights, c, chunks, mixed)
        else:
            mixed, *kept = forward_many(blk, parts, *weights)
        saved.append(kept)
    mixed_back = exchange(after(mixed, g))

    g = after(g, mixed)
    for c in range(chunks):
        if small:
            keep, give = backward(blk, *saved[c], g, *weights, c)
        else:
            keep, give = backward_many(blk, *saved[c], g, *weights)
        keep, got, partial = reduce_pairs(keep, give)
        g = after(g, partial)
        before_last = partial
        if c > 0:
            partial = after(partial, saved[c - 1][3])
        saved[c] = (keep, *got, swap(partial, 2))
    back, last = ([], mixed_back)
    for c in range(chunks):
        last = exchange(after(add(*saved[c]), last, before_last))
        back.append(last)
        if c == 0:
            keep, give = project_out(blk, slot_col, w_out, mixed_back)
            keep, got, before_last = reduce_pairs(keep, give)
            attended = add(keep, *got, swap(before_last, 2))
    return (attended, to_tokens(slot_col, back))


def solution(mesh):
    in_specs = (
        P("seq", "tp"),
        P("seq", None),
        P(None, "tp"),
        P(None, "tp"),
        P(None, "tp"),
        P("tp", None),
        P("seq", "tp"),
    )
    out_specs = (P("seq", "tp"), P("seq", "tp"))
    return jax.shard_map(body, mesh=mesh, in_specs=in_specs, out_specs=out_specs, check_vma=False)
```

```python
import functools
import jax
import jax.numpy as jnp
from jax import lax
from jax.experimental import pallas as pl
from jax.experimental.pallas import tpu as pltpu
from jax.sharding import PartitionSpec as P

HEAD_DIM = 128
CLUSTERS = 128
CAP = 256
MOST = 8
LIMIT = 24.0
EMPTY = 32.0
NN = (((1,), (0,)), ((), ()))
NT = (((1,), (1,)), ((), ()))
TN = (((0,), (0,)), ((), ()))
MB = 1024 * 1024
CHUNKS = 2
GRANT = 50 * MB


def cost(giga):
    return pl.CostEstimate(flops=int(giga * 1e9), bytes_accessed=MB, transcendentals=0)


VMEM = pl.BlockSpec(memory_space=pltpu.VMEM)
SMEM = pl.BlockSpec(memory_space=pltpu.SMEM)


def dot(a, b, dims=NN):
    return lax.dot_general(a, b, dims, preferred_element_type=jnp.float32)


def iota(shape, dim):
    return lax.broadcasted_iota(jnp.int32, shape, dim)


def swap(x, bit):
    count = lax.axis_size("tp")
    return lax.ppermute(x, "tp", [(i, i ^ bit) for i in range(count)])


def exchange(x):
    return lax.all_to_all(x, "seq", split_axis=0, concat_axis=0, tiled=True)


def after(x, *others):
    return lax.optimization_barrier((x,) + others)[0]


def slots_of(out, tokens, chunk, chunks):
    owners, rows, _ = out.shape
    shape = (owners, rows, tokens)
    slot = iota(shape, 0) * (rows * chunks) + iota(shape, 1) + chunk * rows
    return slot.reshape(owners * rows, tokens)


def put_rows(slot_row, x_ref, out, chunk, chunks):
    tokens = x_ref.shape[0]
    held = slots_of(out, tokens, chunk, chunks) == slot_row
    chosen = jnp.where(held, 1.0, 0.0)
    taken = jnp.sum(chosen, axis=1, keepdims=True)
    value = dot(chosen.astype(jnp.bfloat16), x_ref[...])
    first = iota(value.shape, 1) == 0
    value = value + jnp.where(first & (taken == 0.0), EMPTY, 0.0)
    out[...] = value.astype(jnp.bfloat16).reshape(out.shape)


def place_kernel(chunks, ids_row, x_ref, slot_col, slot_row, out):
    tokens = x_ref.shape[0]
    here, there = (iota((tokens, tokens), 0), iota((tokens, tokens), 1))
    row = ids_row[...]
    col = jnp.sum(jnp.where(here == there, row, 0), axis=1, keepdims=True)
    same = col == row
    earlier = jnp.where(same & (there < here), 1.0, 0.0)
    later = jnp.where(same & (here < there), 1.0, 0.0)
    slot_col[...] = col * MOST + jnp.sum(earlier, axis=1, keepdims=True).astype(jnp.int32)
    rows = row * MOST + jnp.sum(later, axis=0, keepdims=True).astype(jnp.int32)
    slot_row[...] = rows
    put_rows(rows, x_ref, out, 0, chunks)


def place_more_kernel(chunk, chunks, slot_row, x_ref, out):
    put_rows(slot_row[...], x_ref, out, chunk, chunks)


def place(ids_row, x, owners, rows, chunks):
    tokens = x.shape[0]
    piece = jax.ShapeDtypeStruct((owners, rows, x.shape[1]), jnp.bfloat16)
    options = dict(
        compiler_params=pltpu.CompilerParams(vmem_limit_bytes=60 * MB), cost_estimate=cost(1)
    )
    slot_col, slot_row, first = pl.pallas_call(
        functools.partial(place_kernel, chunks),
        out_shape=(
            jax.ShapeDtypeStruct((tokens, 1), jnp.int32),
            jax.ShapeDtypeStruct((1, tokens), jnp.int32),
            piece,
        ),
        name="place",
        **options,
    )(ids_row, x)
    pieces = [first]
    for c in range(1, chunks):
        kernel = functools.partial(place_more_kernel, c, chunks)
        more = pl.pallas_call(kernel, out_shape=piece, name="place_more", **options)
        pieces.append(more(slot_row, x))
    return (slot_col, slot_row, *pieces)


def head_grads_kernel(blk, a0, a1, a2, a3, w_out, slot_row, out_ref):
    width = a0.shape[1]
    total = None
    for j, part in enumerate((a0, a1, a2, a3)):
        cols = pl.ds(pl.multiple_of(blk[j] * width, width), width)
        term = dot(part[...], w_out[:, cols], NT)
        total = term if total is None else total + term
    slots, tokens = (out_ref.shape[0], a0.shape[0])
    chosen = jnp.where(iota((slots, tokens), 0) == slot_row[...], 1.0, 0.0).astype(jnp.bfloat16)
    out_ref[...] = dot(chosen, total.astype(jnp.bfloat16)).astype(jnp.bfloat16)


def head_grads(blk, parts, w_out, slot_row):
    return pl.pallas_call(
        head_grads_kernel,
        out_shape=jax.ShapeDtypeStruct((CLUSTERS * MOST, w_out.shape[0]), jnp.bfloat16),
        in_specs=[SMEM] + [VMEM] * 6,
        out_specs=VMEM,
        compiler_params=pltpu.CompilerParams(vmem_limit_bytes=GRANT),
        cost_estimate=cost(2),
        name="head_grads",
    )(blk, *parts, w_out, slot_row)


GROUP = 16


def spans(blk, width):
    return [pl.ds(pl.multiple_of(blk[j] * width, width), width) for j in range(4)]


def load_all(first, sources, targets, sems):
    @pl.when(first)
    def _():
        for source, target, i in zip(sources, targets, range(3)):
            pltpu.make_async_copy(source, target, sems.at[i]).start()


def wait_for(first, source, target, sem):
    @pl.when(first)
    def _():
        pltpu.make_async_copy(source, target, sem).wait()


def forward_kernel(blk, x0, x1, x2, x3, wq, wk, wv, *refs):
    mixed, saved, probs_ref = refs[-3:]
    sources, rows, width = x0.shape
    heads_width = wq.shape[1]
    heads = heads_width // HEAD_DIM
    scale = HEAD_DIM ** (-0.5)
    span = spans(blk, width)
    members = sources * GROUP
    shape = (sources, GROUP, members)
    here = (iota(shape, 1) // MOST).reshape(members, members)
    source_here = iota(shape, 0).reshape(members, members)
    place_here = iota(shape, 1).reshape(members, members)
    lane = iota((members, members), 1)
    there = lane % GROUP // MOST
    same = here == there
    earlier = same & (lane // GROUP < source_here)
    later = same & (lane // GROUP > source_here)
    diagonal = source_here * GROUP + place_here == lane
    rank_col = (place_here % MOST).astype(jnp.float32)[:, :1]
    rank_row = (lane % MOST).astype(jnp.float32)[:1, :]
    groups = [slice(n * GROUP, (n + 1) * GROUP) for n in range(rows // GROUP)]
    kept, usable = ([], [])
    for group in groups:
        mark = x0[:, group, :HEAD_DIM].reshape(members, HEAD_DIM)[:, :1].astype(jnp.float32)
        held_col = jnp.where(mark <= LIMIT, 1.0, 0.0)
        held_row = jnp.sum(jnp.where(diagonal, held_col, 0.0), axis=0, keepdims=True)
        place_col = rank_col + jnp.sum(jnp.where(earlier, held_row, 0.0), axis=1, keepdims=True)
        place_row = rank_row + jnp.sum(jnp.where(later, held_col, 0.0), axis=0, keepdims=True)
        kept.append(jnp.where(place_col < CAP, held_col, 0.0))
        usable.append(same & (jnp.where(place_row < CAP, held_row, 0.0) > 0))

    xs = [r[...].reshape(sources * rows, width) for r in (x0, x1, x2, x3)]
    for i, w in enumerate((wq, wk, wv)):
        total = dot(xs[0], w[span[0], :])
        for j in range(1, 4):
            total = total + dot(xs[j], w[span[j], :])
        saved[:, :, i * heads_width : (i + 1) * heads_width] = total.astype(jnp.bfloat16).reshape(
            sources, rows, heads_width
        )

    def part(i, n, h):
        start = i * heads_width + h * HEAD_DIM
        return saved[:, groups[n], start : start + HEAD_DIM].reshape(members, HEAD_DIM)

    every = [(n, h) for n in range(len(groups)) for h in range(heads)]
    scores = [
        jnp.where(usable[n], dot(part(0, n, h), part(1, n, h), NT) * scale, -1e30)
        for n, h in every
    ]
    raised = [jnp.exp(s - jnp.max(s, axis=1, keepdims=True)) for s in scores]
    probs = [
        r * (kept[n] / jnp.sum(r, axis=1, keepdims=True)) for (n, h), r in zip(every, raised)
    ]
    for (n, h), p in zip(every, probs):
        probs_ref[0, n, h] = p
        out = dot(p.astype(jnp.bfloat16), part(2, n, h)).astype(jnp.bfloat16)
        mixed[:, groups[n], h * HEAD_DIM : (h + 1) * HEAD_DIM] = out.reshape(
            sources, GROUP, HEAD_DIM
        )


def backward_kernel(blk, saved, probs_ref, g_ref, wq, wk, wv, *refs):
    keep, give, (dq, dk, dv) = (refs[:2], refs[2:6], refs[6:])
    sources, rows, _ = saved.shape
    width = keep[0].shape[2]
    heads_width = wq.shape[1]
    heads = heads_width // HEAD_DIM
    scale = HEAD_DIM ** (-0.5)
    span = spans(blk, width)
    members = sources * GROUP
    groups = [slice(n * GROUP, (n + 1) * GROUP) for n in range(rows // GROUP)]
    every = [(n, h) for n in range(len(groups)) for h in range(heads)]

    def part(i, n, h):
        start = i * heads_width + h * HEAD_DIM
        return saved[:, groups[n], start : start + HEAD_DIM].reshape(members, HEAD_DIM)

    def grad(n, h):
        return g_ref[:, groups[n], h * HEAD_DIM : (h + 1) * HEAD_DIM].reshape(members, HEAD_DIM)

    def put(ref, n, h, value):
        cols = slice(h * HEAD_DIM, (h + 1) * HEAD_DIM)
        ref[:, groups[n], cols] = value.astype(jnp.bfloat16).reshape(sources, GROUP, HEAD_DIM)

    grad_probs = [dot(grad(n, h), part(2, n, h), NT) for n, h in every]
    for n, h in every:
        put(dv, n, h, dot(probs_ref[0, n, h].astype(jnp.bfloat16), grad(n, h), TN))
    inner = [
        jnp.sum(gp * probs_ref[0, n, h], axis=1, keepdims=True)
        for (n, h), gp in zip(every, grad_probs)
    ]
    grad_scores = [
        (probs_ref[0, n, h] * (gp - i) * scale).astype(jnp.bfloat16)
        for (n, h), gp, i in zip(every, grad_probs, inner)
    ]
    for (n, h), gs in zip(every, grad_scores):
        put(dq, n, h, dot(gs, part(1, n, h)))
    for (n, h), gs in zip(every, grad_scores):
        put(dk, n, h, dot(gs, part(0, n, h), TN))
    grads = [d[...].reshape(sources * rows, heads_width) for d in (dq, dk, dv)]
    for j in (1, 3, 0, 2):
        total = None
        for d, w in zip(grads, (wq, wk, wv)):
            term = dot(d, w[span[j], :], NT)
            total = term if total is None else total + term
        total = total.astype(jnp.bfloat16).reshape(sources, rows, width)
        if j % 2 == 0:
            keep[j // 2][...] = total
        else:
            give[j - 1][...] = total[: sources // 2]
            give[j][...] = total[sources // 2 :]


def step_of(sources, rows):
    step = GROUP
    while step * 2 * sources <= 512 and rows % (step * 2) == 0:
        step *= 2
    return step


def forward(blk, parts, wq, wk, wv, chunk, chunks, mixed):
    sources, rows, width = parts[2].shape
    heads_width = wq.shape[1]
    heads = heads_width // HEAD_DIM
    step = step_of(sources, rows)
    steps, groups, members = (rows // step, step // GROUP, sources * GROUP)
    block = pl.BlockSpec((sources, step, width), lambda p: (0, p, 0))
    weight = VMEM
    in_specs = [SMEM] + [block] * 4 + [weight] * 3
    operands = [blk, *parts, wq, wk, wv]
    if mixed is not None:
        in_specs.append(pl.BlockSpec(memory_space=pl.ANY))
        operands.append(mixed)
    return pl.pallas_call(
        forward_kernel,
        grid=(steps,),
        out_shape=(
            jax.ShapeDtypeStruct((sources, rows * chunks, heads_width), jnp.bfloat16),
            jax.ShapeDtypeStruct((sources, rows, 3 * heads_width), jnp.bfloat16),
            jax.ShapeDtypeStruct((steps, groups, heads, members, members), jnp.float32),
        ),
        in_specs=in_specs,
        out_specs=(
            pl.BlockSpec((sources, step, heads_width), lambda p: (0, p + chunk * steps, 0)),
            pl.BlockSpec((sources, step, 3 * heads_width), lambda p: (0, p, 0)),
            pl.BlockSpec((1, groups, heads, members, members), lambda p: (p, 0, 0, 0, 0)),
        ),
        input_output_aliases={} if mixed is None else {len(operands) - 1: 0},
        compiler_params=pltpu.CompilerParams(vmem_limit_bytes=40 * MB),
        cost_estimate=cost(2),
        name="forward",
    )(*operands)


def backward(blk, saved, probs, grads, wq, wk, wv, chunk):
    sources, rows, _ = saved.shape
    heads_width = wq.shape[1]
    width = wq.shape[0] // 4
    heads = heads_width // HEAD_DIM
    step = step_of(sources, rows)
    steps, groups, members = (rows // step, step // GROUP, sources * GROUP)
    block = pl.BlockSpec((sources, step, width), lambda p: (0, p, 0))
    half = pl.BlockSpec((sources // 2, step, width), lambda p: (0, p, 0))
    weight = VMEM
    shape = jax.ShapeDtypeStruct((sources, rows, width), jnp.bfloat16)
    half_shape = jax.ShapeDtypeStruct((sources // 2, rows, width), jnp.bfloat16)
    outs = pl.pallas_call(
        backward_kernel,
        grid=(steps,),
        out_shape=(shape,) * 2 + (half_shape,) * 4,
        in_specs=[
            SMEM,
            pl.BlockSpec((sources, step, 3 * heads_width), lambda p: (0, p, 0)),
            pl.BlockSpec((1, groups, heads, members, members), lambda p: (p, 0, 0, 0, 0)),
            pl.BlockSpec((sources, step, heads_width), lambda p: (0, p + chunk * steps, 0)),
            weight,
            weight,
            weight,
        ],
        out_specs=(block,) * 2 + (half,) * 4,
        scratch_shapes=[pltpu.VMEM((sources, step, heads_width), jnp.bfloat16)] * 3,
        compiler_params=pltpu.CompilerParams(vmem_limit_bytes=GRANT),
        cost_estimate=cost(2),
        name="backward",
    )(blk, saved, probs, grads, wq, wk, wv)
    return (outs[:2], outs[2:])


def slab(w, blk, j):
    width = w.shape[0] // 4
    return lax.dynamic_slice_in_dim(w, blk[j] * width, width, 0)


def by_cluster(x):
    sources, rows = x.shape[:2]
    x = x.reshape(sources, rows // MOST, MOST, -1).transpose(1, 0, 2, 3)
    return x.reshape(rows // MOST, sources * MOST, -1)


def by_source(x, sources):
    clusters = x.shape[0]
    x = x.reshape(clusters, sources, MOST, -1).transpose(1, 0, 2, 3)
    return x.reshape(sources, clusters * MOST, -1)


def split_heads(x):
    return x.reshape(x.shape[0], -1, HEAD_DIM)


ein = functools.partial(jnp.einsum, preferred_element_type=jnp.float32)


def forward_many(blk, parts, wq, wk, wv):
    sources, rows, _ = parts[0].shape

    def project(w):
        total = 0.0
        for j in range(4):
            total = total + ein("srd,dh->srh", parts[j], slab(w, blk, j))
        return by_cluster(total.astype(jnp.bfloat16))

    held = (parts[0][:, :, 0].astype(jnp.float32) <= LIMIT).reshape(sources, -1, MOST)
    counts = jnp.sum(held.astype(jnp.int32), axis=2, keepdims=True)
    rank = jnp.cumsum(counts, axis=0) - counts + jnp.arange(MOST)
    kept = by_cluster((held & (rank < CAP)).astype(jnp.float32).reshape(sources, rows, 1))
    scale = HEAD_DIM ** (-0.5)

    def one(args):
        q, k, v, live = args
        q, k, v = (split_heads(a) for a in (q, k, v))
        scores = jnp.where(live[None, None, :, 0] > 0, ein("qhd,khd->hqk", q, k) * scale, -1e30)
        raised = jnp.exp(scores - jnp.max(scores, axis=-1, keepdims=True))
        probs = raised * (live / jnp.sum(raised, axis=-1, keepdims=True))
        mixed = ein("hqk,khd->qhd", probs.astype(jnp.bfloat16), v).astype(jnp.bfloat16)
        return (mixed.reshape(mixed.shape[0], -1), probs)

    saved = tuple(project(w) for w in (wq, wk, wv))
    mixed, probs = lax.map(one, saved + (kept,))
    return (by_source(mixed, sources), saved, probs)


def backward_many(blk, saved, probs, grads, wq, wk, wv):
    sources = grads.shape[0]
    scale = HEAD_DIM ** (-0.5)

    def one(args):
        q, k, v, probs, g = args
        q, k, v, g = (split_heads(a) for a in (q, k, v, g))
        dv = ein("hqk,qhd->khd", probs.astype(jnp.bfloat16), g)
        grad_probs = ein("qhd,khd->hqk", g, v)
        inner = jnp.sum(grad_probs * probs, axis=-1, keepdims=True)
        grad_scores = (probs * (grad_probs - inner) * scale).astype(jnp.bfloat16)
        dq = ein("hqk,khd->qhd", grad_scores, k)
        dk = ein("hqk,qhd->khd", grad_scores, q)
        return tuple(a.astype(jnp.bfloat16).reshape(a.shape[0], -1) for a in (dq, dk, dv))

    dq, dk, dv = lax.map(one, saved + (probs, by_cluster(grads)))
    outs = []
    for j in range(4):
        total = 0.0
        for d, w in ((dq, wq), (dk, wk), (dv, wv)):
            total = total + ein("crh,wh->crw", d, slab(w, blk, j))
        outs.append(by_source(total.astype(jnp.bfloat16), sources))
    half = sources // 2
    return ((outs[0], outs[2]), (outs[1][:half], outs[1][half:], outs[3][:half], outs[3][half:]))


def pick(slot_col, parts):
    total = None
    for c, part in enumerate(parts):
        owners, rows, width = part.shape
        i = iota((1, owners * rows), 1)
        slots = i // rows * (rows * len(parts)) + i % rows + c * rows
        chosen = jnp.where(slots == slot_col[...], 1.0, 0.0).astype(jnp.bfloat16)
        term = dot(chosen, part[...].reshape(owners * rows, width))
        total = term if total is None else total + term
    return total


def out_kernel(blk, slot_col, w_out, mixed, *outs):
    keep, give = (outs[:2], outs[2:])
    heads = pick(slot_col, (mixed,)).astype(jnp.bfloat16)
    tokens, width = keep[0].shape
    span = spans(blk, width)
    for j in (1, 3, 0, 2):
        total = dot(heads, w_out[:, span[j]]).astype(jnp.bfloat16)
        if j % 2 == 0:
            keep[j // 2][...] = total
        else:
            give[j - 1][...] = total[: tokens // 2]
            give[j][...] = total[tokens // 2 :]


def project_out(blk, slot_col, w_out, mixed):
    tokens, width = (slot_col.shape[0], w_out.shape[1] // 4)
    shape = jax.ShapeDtypeStruct((tokens, width), jnp.bfloat16)
    half = jax.ShapeDtypeStruct((tokens // 2, width), jnp.bfloat16)
    outs = pl.pallas_call(
        out_kernel,
        out_shape=(shape,) * 2 + (half,) * 4,
        in_specs=[SMEM] + [VMEM] * 3,
        out_specs=(VMEM,) * 6,
        compiler_params=pltpu.CompilerParams(vmem_limit_bytes=GRANT),
        cost_estimate=cost(2),
        name="project_out",
    )(blk, slot_col, w_out, mixed)
    return (outs[:2], outs[2:])


def final_kernel(slot_col, *refs):
    refs[-1][...] = pick(slot_col, refs[:-1])


def to_tokens(slot_col, parts):
    tokens = slot_col.shape[0]
    width = parts[0].shape[2]
    block = tokens
    return pl.pallas_call(
        final_kernel,
        grid=(tokens // block,),
        out_shape=jax.ShapeDtypeStruct((tokens, width), jnp.float32),
        in_specs=[pl.BlockSpec((block, 1), lambda p: (p, 0))]
        + [pl.BlockSpec(parts[0].shape, lambda p: (0, 0, 0))] * len(parts),
        out_specs=pl.BlockSpec((block, width), lambda p: (p, 0)),
        compiler_params=pltpu.CompilerParams(vmem_limit_bytes=GRANT),
        cost_estimate=cost(1),
        name="to_tokens",
    )(slot_col, *parts)


def wide(x):
    return x.astype(jnp.float32)


def add_kernel(*refs):
    whole, halves, more, out = (refs[0], refs[1:3], refs[3:-1], refs[-1])
    size = whole.shape[0] // 2
    for i, half in enumerate(halves):
        rows = slice(i * size, (i + 1) * size)
        total = wide(whole[rows]) + wide(half[...])
        if more:
            total = total + wide(more[0][rows])
        out[rows] = total.astype(jnp.bfloat16)


def add(whole, first, second, *more, into=None, chunk=0, chunks=1):
    shape = whole.shape
    block = pl.BlockSpec(shape, lambda p: (0,) * len(shape))
    half = pl.BlockSpec(first.shape, lambda p: (0,) * len(shape))
    place = (0, chunk, 0)[: len(shape)]
    full = (shape[0], shape[1] * chunks) + shape[2:] if chunks > 1 else shape
    operands = [whole, first, second, *more]
    in_specs = [block, half, half] + [block] * len(more)
    kernel, aliases = (add_kernel, {})
    if into is not None:
        aliases = {len(operands): 0}
        operands.append(into)
        in_specs.append(pl.BlockSpec(memory_space=pl.ANY))

        def kernel(*refs):
            add_kernel(*refs[:-2], refs[-1])

    return pl.pallas_call(
        kernel,
        grid=(1,),
        out_shape=jax.ShapeDtypeStruct(full, jnp.bfloat16),
        in_specs=in_specs,
        out_specs=pl.BlockSpec(shape, lambda p: place if chunks > 1 else (0,) * len(shape)),
        input_output_aliases=aliases,
        compiler_params=pltpu.CompilerParams(vmem_limit_bytes=GRANT),
        cost_estimate=cost(0.001),
        name="add",
    )(*operands)


def reduce_pairs(keep, give):
    got = [swap(x, 1) for x in give]
    return (keep[0], got[:2], add(keep[1], *got[2:]))


def body(normed, cluster, w_query, w_key, w_value, w_out, grad_out):
    seq_count = lax.axis_size("seq")
    per = CLUSTERS // seq_count * MOST
    chunks = CHUNKS if per // CHUNKS % GROUP == 0 else 1
    rows = per // chunks
    blk = lax.axis_index("tp") ^ jnp.arange(4, dtype=jnp.int32)
    weights = (w_query, w_key, w_value)
    small = seq_count * GROUP <= 256

    g_across = swap(grad_out, 2)
    g_parts = (grad_out, swap(grad_out, 1), g_across, swap(g_across, 1))
    slot_col, slot_row, *pieces = place(cluster.reshape(1, -1), normed, seq_count, rows, chunks)
    xs, x_across = ([], [])
    for piece in pieces:
        xs.append(exchange(after(piece, *xs[-1:])))
    for x in xs:
        x_across.append(swap(x, 2))
    g_slots = head_grads(blk, g_parts, w_out, slot_row).reshape(seq_count, per, -1)
    g = exchange(after(g_slots, xs[-1], x_across[0]))

    mixed, saved = (None, [])
    for c in range(chunks):
        if c > 0:
            x_across[c] = after(x_across[c], mixed)
        parts = (xs[c], swap(xs[c], 1), x_across[c], swap(x_across[c], 1))
        if small:
            mixed, *kept = forward(blk, parts, *weights, c, chunks, mixed)
        else:
            mixed, *kept = forward_many(blk, parts, *weights)
        saved.append(kept)
    mixed_back = exchange(after(mixed, g))

    g = after(g, mixed)
    for c in range(chunks):
        if small:
            keep, give = backward(blk, *saved[c], g, *weights, c)
        else:
            keep, give = backward_many(blk, *saved[c], g, *weights)
        keep, got, partial = reduce_pairs(keep, give)
        g = after(g, partial)
        before_last = partial
        if c > 0:
            partial = after(partial, saved[c - 1][3])
        saved[c] = (keep, *got, swap(partial, 2))
    back, last = ([], mixed_back)
    for c in range(chunks):
        last = exchange(after(add(*saved[c]), last, before_last))
        back.append(last)
        if c == 0:
            keep, give = project_out(blk, slot_col, w_out, mixed_back)
            keep, got, before_last = reduce_pairs(keep, give)
            attended = add(keep, *got, swap(before_last, 2))
    return (attended, to_tokens(slot_col, back))


def solution(mesh):
    in_specs = (
        P("seq", "tp"),
        P("seq", None),
        P(None, "tp"),
        P(None, "tp"),
        P(None, "tp"),
        P("tp", None),
        P("seq", "tp"),
    )
    out_specs = (P("seq", "tp"), P("seq", "tp"))
    return jax.shard_map(body, mesh=mesh, in_specs=in_specs, out_specs=out_specs, check_vma=False)
```

```python
import functools
import jax
import jax.numpy as jnp
from jax import lax
from jax.experimental import pallas as pl
from jax.experimental.pallas import tpu as pltpu
from jax.sharding import PartitionSpec as P

HEAD_DIM = 128
CLUSTERS = 128
CAP = 256
MOST = 8
LIMIT = 24.0
EMPTY = 32.0
NN = (((1,), (0,)), ((), ()))
NT = (((1,), (1,)), ((), ()))
TN = (((0,), (0,)), ((), ()))
MB = 1024 * 1024
CHUNKS = 2
GRANT = 50 * MB


def cost(giga):
    return pl.CostEstimate(flops=int(giga * 1e9), bytes_accessed=MB, transcendentals=0)


VMEM = pl.BlockSpec(memory_space=pltpu.VMEM)
SMEM = pl.BlockSpec(memory_space=pltpu.SMEM)


def dot(a, b, dims=NN):
    return lax.dot_general(a, b, dims, preferred_element_type=jnp.float32)


def iota(shape, dim):
    return lax.broadcasted_iota(jnp.int32, shape, dim)


def swap(x, bit):
    count = lax.axis_size("tp")
    return lax.ppermute(x, "tp", [(i, i ^ bit) for i in range(count)])


def exchange(x):
    return lax.all_to_all(x, "seq", split_axis=0, concat_axis=0, tiled=True)


def after(x, *others):
    return lax.optimization_barrier((x,) + others)[0]


def slots_of(out, tokens, chunk, chunks):
    owners, rows, _ = out.shape
    shape = (owners, rows, tokens)
    slot = iota(shape, 0) * (rows * chunks) + iota(shape, 1) + chunk * rows
    return slot.reshape(owners * rows, tokens)


def put_rows(slot_row, x_ref, out, chunk, chunks):
    tokens = x_ref.shape[0]
    held = slots_of(out, tokens, chunk, chunks) == slot_row
    chosen = jnp.where(held, 1.0, 0.0)
    taken = jnp.sum(chosen, axis=1, keepdims=True)
    value = dot(chosen.astype(jnp.bfloat16), x_ref[...])
    first = iota(value.shape, 1) == 0
    value = value + jnp.where(first & (taken == 0.0), EMPTY, 0.0)
    out[...] = value.astype(jnp.bfloat16).reshape(out.shape)


def place_kernel(chunks, ids_row, x_ref, slot_col, slot_row, out):
    tokens = x_ref.shape[0]
    here, there = (iota((tokens, tokens), 0), iota((tokens, tokens), 1))
    row = ids_row[...]
    col = jnp.sum(jnp.where(here == there, row, 0), axis=1, keepdims=True)
    same = col == row
    earlier = jnp.where(same & (there < here), 1.0, 0.0)
    later = jnp.where(same & (here < there), 1.0, 0.0)
    slot_col[...] = col * MOST + jnp.sum(earlier, axis=1, keepdims=True).astype(jnp.int32)
    rows = row * MOST + jnp.sum(later, axis=0, keepdims=True).astype(jnp.int32)
    slot_row[...] = rows
    put_rows(rows, x_ref, out, 0, chunks)


def place_more_kernel(chunk, chunks, slot_row, x_ref, out):
    put_rows(slot_row[...], x_ref, out, chunk, chunks)


def place(ids_row, x, owners, rows, chunks):
    tokens = x.shape[0]
    piece = jax.ShapeDtypeStruct((owners, rows, x.shape[1]), jnp.bfloat16)
    options = dict(
        compiler_params=pltpu.CompilerParams(vmem_limit_bytes=60 * MB), cost_estimate=cost(1)
    )
    slot_col, slot_row, first = pl.pallas_call(
        functools.partial(place_kernel, chunks),
        out_shape=(
            jax.ShapeDtypeStruct((tokens, 1), jnp.int32),
            jax.ShapeDtypeStruct((1, tokens), jnp.int32),
            piece,
        ),
        name="place",
        **options,
    )(ids_row, x)
    pieces = [first]
    for c in range(1, chunks):
        kernel = functools.partial(place_more_kernel, c, chunks)
        more = pl.pallas_call(kernel, out_shape=piece, name="place_more", **options)
        pieces.append(more(slot_row, x))
    return (slot_col, slot_row, *pieces)


def head_grads_kernel(blk, a0, a1, a2, a3, w_out, slot_row, out_ref):
    width = a0.shape[1]
    total = None
    for j, part in enumerate((a0, a1, a2, a3)):
        cols = pl.ds(pl.multiple_of(blk[j] * width, width), width)
        term = dot(part[...], w_out[:, cols], NT)
        total = term if total is None else total + term
    slots, tokens = (out_ref.shape[0], a0.shape[0])
    chosen = jnp.where(iota((slots, tokens), 0) == slot_row[...], 1.0, 0.0).astype(jnp.bfloat16)
    out_ref[...] = dot(chosen, total.astype(jnp.bfloat16)).astype(jnp.bfloat16)


def head_grads(blk, parts, w_out, slot_row):
    return pl.pallas_call(
        head_grads_kernel,
        out_shape=jax.ShapeDtypeStruct((CLUSTERS * MOST, w_out.shape[0]), jnp.bfloat16),
        in_specs=[SMEM] + [VMEM] * 6,
        out_specs=VMEM,
        compiler_params=pltpu.CompilerParams(vmem_limit_bytes=GRANT),
        cost_estimate=cost(2),
        name="head_grads",
    )(blk, *parts, w_out, slot_row)


GROUP = 16


def spans(blk, width):
    return [pl.ds(pl.multiple_of(blk[j] * width, width), width) for j in range(4)]


def load_all(first, sources, targets, sems):
    @pl.when(first)
    def _():
        for source, target, i in zip(sources, targets, range(3)):
            pltpu.make_async_copy(source, target, sems.at[i]).start()


def wait_for(first, source, target, sem):
    @pl.when(first)
    def _():
        pltpu.make_async_copy(source, target, sem).wait()


def forward_kernel(blk, x0, x1, x2, x3, wq, wk, wv, *refs):
    mixed, saved, probs_ref = refs[-3:]
    sources, rows, width = x0.shape
    heads_width = wq.shape[1]
    heads = heads_width // HEAD_DIM
    scale = HEAD_DIM ** (-0.5)
    span = spans(blk, width)
    members = sources * GROUP
    shape = (sources, GROUP, members)
    here = (iota(shape, 1) // MOST).reshape(members, members)
    source_here = iota(shape, 0).reshape(members, members)
    place_here = iota(shape, 1).reshape(members, members)
    lane = iota((members, members), 1)
    there = lane % GROUP // MOST
    same = here == there
    earlier = same & (lane // GROUP < source_here)
    later = same & (lane // GROUP > source_here)
    diagonal = source_here * GROUP + place_here == lane
    rank_col = (place_here % MOST).astype(jnp.float32)[:, :1]
    rank_row = (lane % MOST).astype(jnp.float32)[:1, :]
    groups = [slice(n * GROUP, (n + 1) * GROUP) for n in range(rows // GROUP)]
    kept, usable = ([], [])
    for group in groups:
        mark = x0[:, group, :HEAD_DIM].reshape(members, HEAD_DIM)[:, :1].astype(jnp.float32)
        held_col = jnp.where(mark <= LIMIT, 1.0, 0.0)
        held_row = jnp.sum(jnp.where(diagonal, held_col, 0.0), axis=0, keepdims=True)
        place_col = rank_col + jnp.sum(jnp.where(earlier, held_row, 0.0), axis=1, keepdims=True)
        place_row = rank_row + jnp.sum(jnp.where(later, held_col, 0.0), axis=0, keepdims=True)
        kept.append(jnp.where(place_col < CAP, held_col, 0.0))
        usable.append(same & (jnp.where(place_row < CAP, held_row, 0.0) > 0))

    xs = [r[...].reshape(sources * rows, width) for r in (x0, x1, x2, x3)]
    for i, w in enumerate((wq, wk, wv)):
        total = dot(xs[0], w[span[0], :])
        for j in range(1, 4):
            total = total + dot(xs[j], w[span[j], :])
        saved[:, :, i * heads_width : (i + 1) * heads_width] = total.astype(jnp.bfloat16).reshape(
            sources, rows, heads_width
        )

    def part(i, n, h):
        start = i * heads_width + h * HEAD_DIM
        return saved[:, groups[n], start : start + HEAD_DIM].reshape(members, HEAD_DIM)

    every = [(n, h) for n in range(len(groups)) for h in range(heads)]
    scores = [
        jnp.where(usable[n], dot(part(0, n, h), part(1, n, h), NT) * scale, -1e30)
        for n, h in every
    ]
    raised = [jnp.exp(s - jnp.max(s, axis=1, keepdims=True)) for s in scores]
    probs = [
        r * (kept[n] / jnp.sum(r, axis=1, keepdims=True)) for (n, h), r in zip(every, raised)
    ]
    for (n, h), p in zip(every, probs):
        probs_ref[0, n, h] = p
        out = dot(p.astype(jnp.bfloat16), part(2, n, h)).astype(jnp.bfloat16)
        mixed[:, groups[n], h * HEAD_DIM : (h + 1) * HEAD_DIM] = out.reshape(
            sources, GROUP, HEAD_DIM
        )


def backward_kernel(blk, saved, probs_ref, g_ref, wq, wk, wv, *refs):
    keep, give, (dq, dk, dv) = (refs[:2], refs[2:6], refs[6:])
    sources, rows, _ = saved.shape
    width = keep[0].shape[2]
    heads_width = wq.shape[1]
    heads = heads_width // HEAD_DIM
    scale = HEAD_DIM ** (-0.5)
    span = spans(blk, width)
    members = sources * GROUP
    groups = [slice(n * GROUP, (n + 1) * GROUP) for n in range(rows // GROUP)]
    every = [(n, h) for n in range(len(groups)) for h in range(heads)]

    def part(i, n, h):
        start = i * heads_width + h * HEAD_DIM
        return saved[:, groups[n], start : start + HEAD_DIM].reshape(members, HEAD_DIM)

    def grad(n, h):
        return g_ref[:, groups[n], h * HEAD_DIM : (h + 1) * HEAD_DIM].reshape(members, HEAD_DIM)

    def put(ref, n, h, value):
        cols = slice(h * HEAD_DIM, (h + 1) * HEAD_DIM)
        ref[:, groups[n], cols] = value.astype(jnp.bfloat16).reshape(sources, GROUP, HEAD_DIM)

    grad_probs = [dot(grad(n, h), part(2, n, h), NT) for n, h in every]
    for n, h in every:
        put(dv, n, h, dot(probs_ref[0, n, h].astype(jnp.bfloat16), grad(n, h), TN))
    inner = [
        jnp.sum(gp * probs_ref[0, n, h], axis=1, keepdims=True)
        for (n, h), gp in zip(every, grad_probs)
    ]
    grad_scores = [
        (probs_ref[0, n, h] * (gp - i) * scale).astype(jnp.bfloat16)
        for (n, h), gp, i in zip(every, grad_probs, inner)
    ]
    for (n, h), gs in zip(every, grad_scores):
        put(dq, n, h, dot(gs, part(1, n, h)))
    for (n, h), gs in zip(every, grad_scores):
        put(dk, n, h, dot(gs, part(0, n, h), TN))
    grads = [d[...].reshape(sources * rows, heads_width) for d in (dq, dk, dv)]
    for j in (1, 3, 0, 2):
        total = None
        for d, w in zip(grads, (wq, wk, wv)):
            term = dot(d, w[span[j], :], NT)
            total = term if total is None else total + term
        total = total.astype(jnp.bfloat16).reshape(sources, rows, width)
        if j % 2 == 0:
            keep[j // 2][...] = total
        else:
            give[j - 1][...] = total[: sources // 2]
            give[j][...] = total[sources // 2 :]


def step_of(sources, rows):
    step = GROUP
    while step * 2 * sources <= 512 and rows % (step * 2) == 0:
        step *= 2
    return step


def forward(blk, parts, wq, wk, wv, chunk, chunks, mixed):
    sources, rows, width = parts[2].shape
    heads_width = wq.shape[1]
    heads = heads_width // HEAD_DIM
    step = step_of(sources, rows)
    steps, groups, members = (rows // step, step // GROUP, sources * GROUP)
    block = pl.BlockSpec((sources, step, width), lambda p: (0, p, 0))
    weight = VMEM
    in_specs = [SMEM] + [block] * 4 + [weight] * 3
    operands = [blk, *parts, wq, wk, wv]
    if mixed is not None:
        in_specs.append(pl.BlockSpec(memory_space=pl.ANY))
        operands.append(mixed)
    return pl.pallas_call(
        forward_kernel,
        grid=(steps,),
        out_shape=(
            jax.ShapeDtypeStruct((sources, rows * chunks, heads_width), jnp.bfloat16),
            jax.ShapeDtypeStruct((sources, rows, 3 * heads_width), jnp.bfloat16),
            jax.ShapeDtypeStruct((steps, groups, heads, members, members), jnp.float32),
        ),
        in_specs=in_specs,
        out_specs=(
            pl.BlockSpec((sources, step, heads_width), lambda p: (0, p + chunk * steps, 0)),
            pl.BlockSpec((sources, step, 3 * heads_width), lambda p: (0, p, 0)),
            pl.BlockSpec((1, groups, heads, members, members), lambda p: (p, 0, 0, 0, 0)),
        ),
        input_output_aliases={} if mixed is None else {len(operands) - 1: 0},
        compiler_params=pltpu.CompilerParams(vmem_limit_bytes=40 * MB),
        cost_estimate=cost(2),
        name="forward",
    )(*operands)


def backward(blk, saved, probs, grads, wq, wk, wv, chunk):
    sources, rows, _ = saved.shape
    heads_width = wq.shape[1]
    width = wq.shape[0] // 4
    heads = heads_width // HEAD_DIM
    step = step_of(sources, rows)
    steps, groups, members = (rows // step, step // GROUP, sources * GROUP)
    block = pl.BlockSpec((sources, step, width), lambda p: (0, p, 0))
    half = pl.BlockSpec((sources // 2, step, width), lambda p: (0, p, 0))
    weight = VMEM
    shape = jax.ShapeDtypeStruct((sources, rows, width), jnp.bfloat16)
    half_shape = jax.ShapeDtypeStruct((sources // 2, rows, width), jnp.bfloat16)
    outs = pl.pallas_call(
        backward_kernel,
        grid=(steps,),
        out_shape=(shape,) * 2 + (half_shape,) * 4,
        in_specs=[
            SMEM,
            pl.BlockSpec((sources, step, 3 * heads_width), lambda p: (0, p, 0)),
            pl.BlockSpec((1, groups, heads, members, members), lambda p: (p, 0, 0, 0, 0)),
            pl.BlockSpec((sources, step, heads_width), lambda p: (0, p + chunk * steps, 0)),
            weight,
            weight,
            weight,
        ],
        out_specs=(block,) * 2 + (half,) * 4,
        scratch_shapes=[pltpu.VMEM((sources, step, heads_width), jnp.bfloat16)] * 3,
        compiler_params=pltpu.CompilerParams(vmem_limit_bytes=GRANT),
        cost_estimate=cost(2),
        name="backward",
    )(blk, saved, probs, grads, wq, wk, wv)
    return (outs[:2], outs[2:])


def slab(w, blk, j):
    width = w.shape[0] // 4
    return lax.dynamic_slice_in_dim(w, blk[j] * width, width, 0)


def by_cluster(x):
    sources, rows = x.shape[:2]
    x = x.reshape(sources, rows // MOST, MOST, -1).transpose(1, 0, 2, 3)
    return x.reshape(rows // MOST, sources * MOST, -1)


def by_source(x, sources):
    clusters = x.shape[0]
    x = x.reshape(clusters, sources, MOST, -1).transpose(1, 0, 2, 3)
    return x.reshape(sources, clusters * MOST, -1)


def split_heads(x):
    return x.reshape(x.shape[0], -1, HEAD_DIM)


ein = functools.partial(jnp.einsum, preferred_element_type=jnp.float32)


def forward_many(blk, parts, wq, wk, wv):
    sources, rows, _ = parts[0].shape

    def project(w):
        total = 0.0
        for j in range(4):
            total = total + ein("srd,dh->srh", parts[j], slab(w, blk, j))
        return by_cluster(total.astype(jnp.bfloat16))

    held = (parts[0][:, :, 0].astype(jnp.float32) <= LIMIT).reshape(sources, -1, MOST)
    counts = jnp.sum(held.astype(jnp.int32), axis=2, keepdims=True)
    rank = jnp.cumsum(counts, axis=0) - counts + jnp.arange(MOST)
    kept = by_cluster((held & (rank < CAP)).astype(jnp.float32).reshape(sources, rows, 1))
    scale = HEAD_DIM ** (-0.5)

    def one(args):
        q, k, v, live = args
        q, k, v = (split_heads(a) for a in (q, k, v))
        scores = jnp.where(live[None, None, :, 0] > 0, ein("qhd,khd->hqk", q, k) * scale, -1e30)
        raised = jnp.exp(scores - jnp.max(scores, axis=-1, keepdims=True))
        probs = raised * (live / jnp.sum(raised, axis=-1, keepdims=True))
        mixed = ein("hqk,khd->qhd", probs.astype(jnp.bfloat16), v).astype(jnp.bfloat16)
        return (mixed.reshape(mixed.shape[0], -1), probs)

    saved = tuple(project(w) for w in (wq, wk, wv))
    mixed, probs = lax.map(one, saved + (kept,))
    return (by_source(mixed, sources), saved, probs)


def backward_many(blk, saved, probs, grads, wq, wk, wv):
    sources = grads.shape[0]
    scale = HEAD_DIM ** (-0.5)

    def one(args):
        q, k, v, probs, g = args
        q, k, v, g = (split_heads(a) for a in (q, k, v, g))
        dv = ein("hqk,qhd->khd", probs.astype(jnp.bfloat16), g)
        grad_probs = ein("qhd,khd->hqk", g, v)
        inner = jnp.sum(grad_probs * probs, axis=-1, keepdims=True)
        grad_scores = (probs * (grad_probs - inner) * scale).astype(jnp.bfloat16)
        dq = ein("hqk,khd->qhd", grad_scores, k)
        dk = ein("hqk,qhd->khd", grad_scores, q)
        return tuple(a.astype(jnp.bfloat16).reshape(a.shape[0], -1) for a in (dq, dk, dv))

    dq, dk, dv = lax.map(one, saved + (probs, by_cluster(grads)))
    outs = []
    for j in range(4):
        total = 0.0
        for d, w in ((dq, wq), (dk, wk), (dv, wv)):
            total = total + ein("crh,wh->crw", d, slab(w, blk, j))
        outs.append(by_source(total.astype(jnp.bfloat16), sources))
    half = sources // 2
    return ((outs[0], outs[2]), (outs[1][:half], outs[1][half:], outs[3][:half], outs[3][half:]))


def pick(slot_col, parts):
    total = None
    for c, part in enumerate(parts):
        owners, rows, width = part.shape
        i = iota((1, owners * rows), 1)
        slots = i // rows * (rows * len(parts)) + i % rows + c * rows
        chosen = jnp.where(slots == slot_col[...], 1.0, 0.0).astype(jnp.bfloat16)
        term = dot(chosen, part[...].reshape(owners * rows, width))
        total = term if total is None else total + term
    return total


def out_kernel(blk, slot_col, w_out, mixed, *outs):
    keep, give = (outs[:2], outs[2:])
    heads = pick(slot_col, (mixed,)).astype(jnp.bfloat16)
    tokens, width = keep[0].shape
    span = spans(blk, width)
    for j in (1, 3, 0, 2):
        total = dot(heads, w_out[:, span[j]]).astype(jnp.bfloat16)
        if j % 2 == 0:
            keep[j // 2][...] = total
        else:
            give[j - 1][...] = total[: tokens // 2]
            give[j][...] = total[tokens // 2 :]


def project_out(blk, slot_col, w_out, mixed):
    tokens, width = (slot_col.shape[0], w_out.shape[1] // 4)
    shape = jax.ShapeDtypeStruct((tokens, width), jnp.bfloat16)
    half = jax.ShapeDtypeStruct((tokens // 2, width), jnp.bfloat16)
    outs = pl.pallas_call(
        out_kernel,
        out_shape=(shape,) * 2 + (half,) * 4,
        in_specs=[SMEM] + [VMEM] * 3,
        out_specs=(VMEM,) * 6,
        compiler_params=pltpu.CompilerParams(vmem_limit_bytes=GRANT),
        cost_estimate=cost(2),
        name="project_out",
    )(blk, slot_col, w_out, mixed)
    return (outs[:2], outs[2:])


def final_kernel(slot_col, *refs):
    refs[-1][...] = pick(slot_col, refs[:-1])


def to_tokens(slot_col, parts):
    tokens = slot_col.shape[0]
    width = parts[0].shape[2]
    block = tokens
    return pl.pallas_call(
        final_kernel,
        grid=(tokens // block,),
        out_shape=jax.ShapeDtypeStruct((tokens, width), jnp.float32),
        in_specs=[pl.BlockSpec((block, 1), lambda p: (p, 0))]
        + [pl.BlockSpec(parts[0].shape, lambda p: (0, 0, 0))] * len(parts),
        out_specs=pl.BlockSpec((block, width), lambda p: (p, 0)),
        compiler_params=pltpu.CompilerParams(vmem_limit_bytes=GRANT),
        cost_estimate=cost(1),
        name="to_tokens",
    )(slot_col, *parts)


def wide(x):
    return x.astype(jnp.float32)


def add_kernel(*refs):
    whole, halves, more, out = (refs[0], refs[1:3], refs[3:-1], refs[-1])
    size = whole.shape[0] // 2
    for i, half in enumerate(halves):
        rows = slice(i * size, (i + 1) * size)
        total = wide(whole[rows]) + wide(half[...])
        if more:
            total = total + wide(more[0][rows])
        out[rows] = total.astype(jnp.bfloat16)


def add(whole, first, second, *more, into=None, chunk=0, chunks=1):
    shape = whole.shape
    block = pl.BlockSpec(shape, lambda p: (0,) * len(shape))
    half = pl.BlockSpec(first.shape, lambda p: (0,) * len(shape))
    place = (0, chunk, 0)[: len(shape)]
    full = (shape[0], shape[1] * chunks) + shape[2:] if chunks > 1 else shape
    operands = [whole, first, second, *more]
    in_specs = [block, half, half] + [block] * len(more)
    kernel, aliases = (add_kernel, {})
    if into is not None:
        aliases = {len(operands): 0}
        operands.append(into)
        in_specs.append(pl.BlockSpec(memory_space=pl.ANY))

        def kernel(*refs):
            add_kernel(*refs[:-2], refs[-1])

    return pl.pallas_call(
        kernel,
        grid=(1,),
        out_shape=jax.ShapeDtypeStruct(full, jnp.bfloat16),
        in_specs=in_specs,
        out_specs=pl.BlockSpec(shape, lambda p: place if chunks > 1 else (0,) * len(shape)),
        input_output_aliases=aliases,
        compiler_params=pltpu.CompilerParams(vmem_limit_bytes=GRANT),
        cost_estimate=cost(0.001),
        name="add",
    )(*operands)


def reduce_pairs(keep, give):
    got = [swap(x, 1) for x in give]
    return (keep[0], got[:2], add(keep[1], *got[2:]))


def body(normed, cluster, w_query, w_key, w_value, w_out, grad_out):
    seq_count = lax.axis_size("seq")
    per = CLUSTERS // seq_count * MOST
    chunks = CHUNKS if per // CHUNKS % GROUP == 0 else 1
    rows = per // chunks
    blk = lax.axis_index("tp") ^ jnp.arange(4, dtype=jnp.int32)
    weights = (w_query, w_key, w_value)
    small = seq_count * GROUP <= 256

    g_across = swap(grad_out, 2)
    g_parts = (grad_out, swap(grad_out, 1), g_across, swap(g_across, 1))
    slot_col, slot_row, *pieces = place(cluster.reshape(1, -1), normed, seq_count, rows, chunks)
    xs, x_across = ([], [])
    for piece in pieces:
        xs.append(exchange(after(piece, *xs[-1:])))
    for x in xs:
        x_across.append(swap(x, 2))
    g_slots = head_grads(blk, g_parts, w_out, slot_row).reshape(seq_count, per, -1)
    g = exchange(after(g_slots, xs[-1]))

    mixed, saved = (None, [])
    for c in range(chunks):
        if c > 0:
            x_across[c] = after(x_across[c], mixed)
        parts = (xs[c], swap(xs[c], 1), x_across[c], swap(x_across[c], 1))
        if small:
            mixed, *kept = forward(blk, parts, *weights, c, chunks, mixed)
        else:
            mixed, *kept = forward_many(blk, parts, *weights)
        saved.append(kept)
    mixed_back = exchange(after(mixed, g))

    g = after(g, mixed)
    for c in range(chunks):
        if small:
            keep, give = backward(blk, *saved[c], g, *weights, c)
        else:
            keep, give = backward_many(blk, *saved[c], g, *weights)
        keep, got, partial = reduce_pairs(keep, give)
        g = after(g, partial)
        before_last = partial
        if c > 0:
            partial = after(partial, saved[c - 1][3])
        saved[c] = (keep, *got, swap(partial, 2))
    back, last = ([], mixed_back)
    for c in range(chunks):
        last = exchange(after(add(*saved[c]), last, before_last))
        back.append(last)
        if c == 0:
            keep, give = project_out(blk, slot_col, w_out, mixed_back)
            keep, got, before_last = reduce_pairs(keep, give)
            attended = add(keep, *got, swap(before_last, 2))
    return (attended, to_tokens(slot_col, back))


def solution(mesh):
    in_specs = (
        P("seq", "tp"),
        P("seq", None),
        P(None, "tp"),
        P(None, "tp"),
        P(None, "tp"),
        P("tp", None),
        P("seq", "tp"),
    )
    out_specs = (P("seq", "tp"), P("seq", "tp"))
    return jax.shard_map(body, mesh=mesh, in_specs=in_specs, out_specs=out_specs, check_vma=False)
```
